128 devices in a mesh: row: 16 (over y, x), col: 8 (over z, core).
Axes of the slice: x: 4, y: 4, z: 4, core: 2. Of those that a mesh axis runs over, the one named last changes fastest.
Arguments:
- amplitudes: bfloat16 [4096, 8, 1024], P('col', None, 'row'), may hold values from -6 to 6
- integrals: bfloat16 [8, 1024, 16384], P(None, 'col', 'row'), may hold values from -0.1875 to 0.1875
- cd_count: int32 [8], replicated, may hold values from 1 to 1024, 6144 in all
- ab_count: int32 [8], replicated, may hold values from 1 to 8192, 49152 in all
Outputs:
- ladder: bfloat16 [4096, 8, 16384], P('col', None, 'row')
The draws below stay inside these ranges and needn't reach their ends.
Inputs may be any that keep to these rules, and one draw needn't show every extreme that they name: `cd_count`: the counts sum to 6144, and the largest is 1024. `ab_count`: the counts sum to 49152, and the largest is 8192.
All inputs are finite; a program needn't handle non-finite values.
Results may differ from the reference program's by a relative error of at most 0.001.
Values may be sent and summed in bfloat16 or wider, within the bound.
A program may use at most 192 MiB of HBM per device.

```python
import math
import jax
import jax.numpy as jnp
import numpy as np
from jax import lax

IRREPS = 8
OCC_ROWS = 4096
CDG = 1024
NABG = 8192
COLUMNS = 16384


def level_of(key, dims, cuts, least, top_value):
    factor_of = 1.0
    for axis_at, blocks in cuts:
        heights = jax.random.uniform(jax.random.fold_in(jax.random.fold_in(key, 6), axis_at), (blocks,), jnp.float32, least / len(cuts), top_value / len(cuts))
        factor_of = factor_of * jnp.repeat(jnp.exp(heights), dims[axis_at] // blocks).reshape((-1,) + (1,) * (len(dims) - 1 - axis_at))
    return factor_of


def profile(number_of, total, bound, skew):
    loads = [(1 << 20) // math.isqrt(standing ** skew) + 1 for standing in range(2, number_of + 1)]
    rest, counts = total - bound - (number_of - 1), [1] * (number_of - 1)
    while rest > 0:
        free = [i for i in range(number_of - 1) if counts[i] < bound]
        mass, budget = sum([loads[i] for i in free]), rest
        for i in free:
            more = min(bound - counts[i], max(1, budget * loads[i] // mass), rest)
            counts[i] = counts[i] + more
            rest = rest - more
    return np.array([bound] + counts)


def ragged_sizes(stream_key, number_of, total, reach, slope):
    if number_of == 2:
        one = jax.random.randint(stream_key, (), max(1, total - reach), min(reach, total - 1) + 1)
        return jnp.stack([one, total - one])
    sizes = jnp.asarray(profile(number_of, total, reach, slope), jnp.int32)
    twos = (number_of - 1) // 2
    source_of, taker = sizes[1:1 + 2 * twos:2], sizes[2:2 + 2 * twos:2]
    slack = jnp.minimum(source_of - 1, reach - taker)
    passed = jax.random.randint(jax.random.fold_in(stream_key, 1), (twos,), 0, 1 << 20) % (slack + 1)
    sizes = sizes.at[1:1 + 2 * twos:2].set(source_of - passed).at[2:2 + 2 * twos:2].set(taker + passed)
    return sizes[jax.random.permutation(jax.random.fold_in(stream_key, 2), number_of)]


def gaussian(own_key, dims, width, bound, shards=(), held_as=jnp.bfloat16):
    values = jax.random.normal(own_key, dims, jnp.float32) * width
    if len(shards) > 0:
        values = level_of(own_key, dims, shards, -0.22, 0.18) * values
    return jnp.clip(values, min=-bound, max=bound).astype(held_as)


def setup_inputs(seed: int = 0) -> dict:
    arg_keys = jax.random.split(jax.random.key(seed), 5)
    return {
        "amplitudes": gaussian(arg_keys[0], (OCC_ROWS, IRREPS, CDG), 1.0, 6.0, ((0, 8), (2, 16))),
        "integrals": gaussian(arg_keys[1], (IRREPS, CDG, COLUMNS), CDG ** -0.5, 0.1875, ((1, 8), (2, 16))),
        "cd_count": ragged_sizes(arg_keys[2], IRREPS, 6 * CDG, CDG, 2).astype(jnp.int32),
        "ab_count": ragged_sizes(arg_keys[3], IRREPS, 6 * NABG, NABG, 2).astype(jnp.int32),
    }


def reference(amplitudes, integrals, cd_count, ab_count):
    slots = lax.broadcasted_iota(jnp.int32, (IRREPS, CDG), 1)
    live = slots < cd_count[:, None]
    live_amps = jnp.where(live[None], amplitudes, jnp.zeros_like(amplitudes))
    places = lax.broadcasted_iota(jnp.int32, (IRREPS, COLUMNS), 1) % NABG
    keep_all = places < ab_count[:, None]

    def one_irrep(index):
        block = lax.dynamic_index_in_dim(live_amps, index, 1, keepdims=False)
        tiles = lax.dynamic_index_in_dim(integrals, index, 0, keepdims=False)
        direct = jnp.dot(block, tiles, preferred_element_type=jnp.float32)
        first = direct[:, :NABG]
        second = direct[:, NABG:]
        joined = jnp.concatenate([first - second, second - first], axis=1)
        keep = lax.dynamic_index_in_dim(keep_all, index, 0, keepdims=False)
        return jnp.where(keep[None], joined, jnp.zeros_like(joined)).astype(jnp.bfloat16)

    result = lax.map(one_irrep, jnp.arange(IRREPS, dtype=jnp.int32))
    return jnp.transpose(result, (1, 0, 2))
```

```python
import functools

import jax
import jax.numpy as jnp
from jax import lax
from jax.experimental import pallas as pl
from jax.experimental.pallas import tpu as pltpu
from jax.sharding import PartitionSpec as P

MESH = pl.DeviceIdType.MESH
IRREPS = 8
PAIRS = 4
SIDE = 4
OCC = 512
DEPTH = 128
WIDTH = 1024
NABG = 8192
TILE = 256
D_KINDS = 8
A_KINDS = 20


def ring(value, step):
    return lax.rem(value + step + SIDE, SIDE)


def kernel(
    cd_ref, ab_ref, amps_ref, ints_ref, out_ref,
    a_all, b_mine, b_other, d_all, peaks, peaks_other, rows_up, scales, a_now, staged,
    b_send, b_recv, d_send, d_recv, a_send, a_recv, s_send, s_recv, here_sem, out_sem,
):
    row, col = lax.axis_index("row"), lax.axis_index("col")
    y, x = row // SIDE, lax.rem(row, SIDE)
    z, core = col // 2, lax.rem(col, 2)
    ids = lambda yy, xx, zz, cc: (yy * SIDE + xx, zz * 2 + cc)
    across = ids(ring(y, 2), x, z, core)
    up_y, down_y = ids(ring(y, 1), x, z, core), ids(ring(y, -1), x, z, core)
    up_x, down_x = ids(y, ring(x, 1), z, core), ids(y, ring(x, -1), z, core)
    up_z, down_z = ids(y, x, ring(z, 1), core), ids(y, x, ring(z, -1), core)
    sibling = ids(y, x, z, 1 - core)
    everyone_z = [ids(y, x, ring(z, s), core) for s in (1, 2, 3)]
    everyone_z += [ids(y, x, ring(z, s), 1 - core) for s in (0, 1, 2, 3)]
    near = [across, up_y, down_y, up_x, down_x, *everyone_z]

    barrier = pltpu.get_barrier_semaphore()
    for device in near:
        pl.semaphore_signal(barrier, inc=1, device_id=device, device_id_type=MESH)
    load_a = pltpu.make_async_copy(amps_ref, a_all.at[:, row], here_sem.at[0])
    load_b = pltpu.make_async_copy(ints_ref, b_mine, here_sem.at[1])
    load_a.start()
    load_b.start()
    pl.semaphore_wait(barrier, len(near))

    def remote(source, target, send, recv, device):
        return pltpu.make_async_remote_copy(
            src_ref=source, dst_ref=target, send_sem=send, recv_sem=recv, device_id=device, device_id_type=MESH
        )

    def b_copy(g):
        return remote(ints_ref.at[g], b_other.at[g], b_send.at[g], b_recv.at[g], across)

    low, high, whole = pl.ds(0, 64), pl.ds(64, 64), pl.ds(0, DEPTH)
    slot = lambda s, c: ring(z, s) * 2 + c
    other = 1 - core
    d_kinds = [
        (slot(0, core), whole, up_z, slot(-1, core)),
        (slot(0, core), whole, down_z, slot(1, core)),
        (slot(0, core), whole, sibling, slot(0, other)),
        (slot(-1, core), low, up_z, slot(2, core)),
        (slot(1, core), high, down_z, slot(2, core)),
        (slot(-1, core), whole, sibling, slot(-1, other)),
        (slot(1, core), whole, sibling, slot(1, other)),
        (slot(2, core), whole, sibling, slot(2, other)),
    ]

    def d_copy(g, kind, arriving=False):
        leaves, rows, device, fills = d_kinds[kind]
        place = d_all.at[g, fills if arriving else leaves, rows]
        return remote(place, place, d_send.at[g, kind], d_recv.at[g, kind], device)

    first, second, every = pl.ds(0, OCC // 2), pl.ds(OCC // 2, OCC // 2), pl.ds(0, OCC)
    block = lambda sy, sx: ring(y, sy) * SIDE + ring(x, sx)
    a_kinds = [
        (block(0, 0), every, up_y, block(-1, 0)),
        (block(0, 0), every, down_y, block(1, 0)),
        (block(-1, 0), first, up_y, block(2, 0)),
        (block(1, 0), second, down_y, block(2, 0)),
    ]
    for sy in (0, -1, 1, 2):
        a_kinds += [
            (block(sy, 0), every, up_x, block(sy, -1)),
            (block(sy, 0), every, down_x, block(sy, 1)),
            (block(sy, -1), first, up_x, block(sy, 2)),
            (block(sy, 1), second, down_x, block(sy, 2)),
        ]

    def a_copy(p, kind, arriving=False):
        leaves, rows, device, fills = a_kinds[kind]
        place = a_all.at[p, fills if arriving else leaves, rows]
        return remote(place, place, a_send.at[p, kind], a_recv.at[p, kind], device)

    def s_copy(n, mine):
        return remote(scales.at[mine], scales.at[mine], s_send.at[n], s_recv.at[n], everyone_z[n])

    def a_own(p):
        for kind in (4, 5, 0, 1):
            a_copy(p, kind).start()

    def a_first(p):
        a_copy(p, 0, True).wait_recv()
        a_copy(p, 2).start()
        a_copy(p, 8).start()
        a_copy(p, 9).start()
        a_copy(p, 1, True).wait_recv()
        a_copy(p, 3).start()
        a_copy(p, 12).start()
        a_copy(p, 13).start()
        a_copy(p, 4, True).wait_recv()
        a_copy(p, 6).start()
        a_copy(p, 5, True).wait_recv()
        a_copy(p, 7).start()

    def a_next(p):
        a_copy(p, 2, True).wait_recv()
        a_copy(p, 3, True).wait_recv()
        a_copy(p, 16).start()
        a_copy(p, 17).start()
        for kind in (8, 9, 12, 13):
            a_copy(p, kind, True).wait_recv()
            a_copy(p, kind + 2).start()

    def a_last(p):
        for kind in (16, 17):
            a_copy(p, kind, True).wait_recv()
            a_copy(p, kind + 2).start()

    def a_end(p):
        for kind in (6, 7, 10, 11, 14, 15, 18, 19):
            a_copy(p, kind, True).wait_recv()

    lane = lax.broadcasted_iota(jnp.int32, (DEPTH, DEPTH), 1)
    depth_at = col * DEPTH + lax.broadcasted_iota(jnp.int32, (DEPTH, WIDTH), 0)
    place_at = lax.rem(row, SIDE * SIDE // 2) * WIDTH + lax.broadcasted_iota(jnp.int32, (DEPTH, WIDTH), 1)

    def form(g):
        b_copy(g).wait_recv()
        ups = jnp.sum(jnp.where(lane == g, rows_up[...], 0.0), axis=1, keepdims=True)
        difference = b_mine[g].astype(jnp.float32) - b_other[g].astype(jnp.float32)
        keep = (depth_at < cd_ref[g]) & (place_at < ab_ref[g])
        scaled = jnp.where(keep, difference * (ups * 32768.0), 0.0)
        whole_number = jnp.round(jnp.minimum(scaled, 32767.0)).astype(jnp.int32)
        d_all[g, col] = whole_number.astype(jnp.int16)
        for kind in (0, 1, 2):
            d_copy(g, kind).start()

    def forward(g):
        d_copy(g, 0, True).wait_recv()
        d_copy(g, 3).start()
        d_copy(g, 5).start()
        d_copy(g, 1, True).wait_recv()
        d_copy(g, 4).start()
        d_copy(g, 6).start()

    def forward_last(g):
        d_copy(g, 3, True).wait_recv()
        d_copy(g, 4, True).wait_recv()
        d_copy(g, 7).start()

    half = lax.broadcasted_iota(jnp.int32, (OCC, 128), 1) < 64

    def out_copy(g, parity):
        return pltpu.make_async_copy(staged.at[parity], out_ref.at[g], out_sem.at[parity])

    def multiply(p, parity):
        g = 2 * p + parity
        for kind in (2, 5, 6, 7):
            d_copy(g, kind, True).wait_recv()
        for m in range(8):
            left, right = a_all[p, 2 * m].astype(jnp.float32), a_all[p, 2 * m + 1].astype(jnp.float32)
            if parity == 0:
                joined = jnp.where(half, left, pltpu.roll(right, 64, 1))
            else:
                joined = jnp.where(half, pltpu.roll(left, 64, 1), right)
            scaled = joined * scales[m, pl.ds(g, 1), :]
            a_now[:, m * 128 : (m + 1) * 128] = scaled.astype(jnp.bfloat16)

        @pl.when(p > 0)
        def _():
            out_copy(g, parity).wait()

        def columns(n, _):
            at = pl.ds(pl.multiple_of(n * TILE, TILE), TILE)
            d = d_all[g, :, :, at].reshape(8 * DEPTH, TILE).astype(jnp.float32)
            top = d.astype(jnp.bfloat16)
            rest = (d - top.astype(jnp.float32)).astype(jnp.bfloat16)
            total = jnp.dot(a_now[...], top, preferred_element_type=jnp.float32)
            total += jnp.dot(a_now[...], rest, preferred_element_type=jnp.float32)
            staged[parity, :, at] = (total * (1.0 / 32768.0)).astype(jnp.bfloat16)
            return 0

        lax.fori_loop(0, WIDTH // TILE, columns, 0)
        out_copy(g, parity).start()

    b_copy(0).start()
    load_a.wait()
    a_copy(0, 4).start()
    a_copy(0, 5).start()
    load_b.wait()

    def peak(g, _):
        size = jnp.abs(b_mine[g].astype(jnp.float32))
        size = jnp.where(place_at < ab_ref[g], size, 0.0)
        most = jnp.max(size, axis=1, keepdims=True)
        peaks[pl.ds(g, 1), :] = jnp.transpose(jnp.broadcast_to(most, (DEPTH, DEPTH)))[0:1, :]
        return 0

    lax.fori_loop(0, IRREPS, peak, 0)
    peak_copy = remote(peaks, peaks_other, s_send.at[7], s_recv.at[7], across)
    peak_copy.start()
    b_copy(1).start()
    a_copy(0, 0).start()
    a_copy(0, 1).start()
    peak_copy.wait_recv()
    left = peaks[...] + peaks_other[...]
    up, down = jnp.ones_like(left), jnp.ones_like(left)
    for power in (32, 16, 8, 4, 2, 1):
        small = left < 2.0**-power
        left = jnp.where(small, left * 2.0**power, left)
        up = jnp.where(small, up * 2.0**power, up)
        down = jnp.where(small, down * 2.0**-power, down)
    rows_up[...] = jnp.transpose(jnp.concatenate([up] * 16, axis=0))
    scales[col] = down
    for n in range(7):
        s_copy(n, col).start()

    def step(p, _):
        for parity in (0, 1):
            g = 2 * p + parity

            @pl.when(g + 2 < IRREPS)
            def _():
                b_copy(g + 2).start()

            @pl.when(g < IRREPS)
            def _():
                form(g)

            if parity == 0:
                @pl.when(p + 1 < PAIRS)
                def _():
                    a_own(p + 1)

                @pl.when(p < PAIRS)
                def _():
                    a_first(p)

                @pl.when((p >= 1) & (p <= PAIRS))
                def _():
                    a_last(p - 1)
            else:
                @pl.when(p < PAIRS)
                def _():
                    a_next(p)

            @pl.when((g >= 1) & (g <= IRREPS))
            def _():
                forward(g - 1)

            @pl.when((g >= 2) & (g <= IRREPS + 1))
            def _():
                forward_last(g - 2)

            if parity == 1:
                @pl.when((p >= 1) & (p <= PAIRS))
                def _():
                    a_end(p - 1)

            @pl.when((g >= 3) & (g <= IRREPS + 2))
            def _():
                multiply((g - 3) // 2, 1 - parity)
        return 0

    step(0, 0)
    for n in range(7):
        sender = [slot(-1, core), slot(-2, core), slot(-3, core)] + [slot(-s, other) for s in (0, 1, 2, 3)]
        s_copy(n, sender[n]).wait_recv()
    lax.fori_loop(1, PAIRS + 2, step, 0)

    for parity in (0, 1):
        out_copy(0, parity).wait()
    for n in range(7):
        s_copy(n, col).wait_send()
    peak_copy.wait_send()

    def drain_b(g, _):
        b_copy(g).wait_send()
        for kind in range(D_KINDS):
            d_copy(g, kind).wait_send()
        return 0

    def drain_a(p, _):
        for kind in range(A_KINDS):
            a_copy(p, kind).wait_send()
        return 0

    lax.fori_loop(0, IRREPS, drain_b, 0)
    lax.fori_loop(0, PAIRS, drain_a, 0)


def per_device(amplitudes, integrals, cd_count, ab_count):
    pairs = amplitudes.reshape(OCC, PAIRS, 128).transpose(1, 0, 2)
    ladder = pl.pallas_call(
        kernel,
        out_shape=jax.ShapeDtypeStruct((IRREPS, OCC, WIDTH), jnp.bfloat16),
        in_specs=[
            pl.BlockSpec(memory_space=pltpu.SMEM),
            pl.BlockSpec(memory_space=pltpu.SMEM),
            pl.BlockSpec(memory_space=pl.ANY),
            pl.BlockSpec(memory_space=pl.ANY),
        ],
        out_specs=pl.BlockSpec(memory_space=pl.ANY),
        scratch_shapes=[
            pltpu.VMEM((PAIRS, 16, OCC, 128), jnp.bfloat16),
            pltpu.VMEM((IRREPS, DEPTH, WIDTH), jnp.bfloat16),
            pltpu.VMEM((IRREPS, DEPTH, WIDTH), jnp.bfloat16),
            pltpu.VMEM((IRREPS, 8, DEPTH, WIDTH), jnp.int16),
            pltpu.VMEM((IRREPS, DEPTH), jnp.float32),
            pltpu.VMEM((IRREPS, DEPTH), jnp.float32),
            pltpu.VMEM((DEPTH, DEPTH), jnp.float32),
            pltpu.VMEM((8, IRREPS, DEPTH), jnp.float32),
            pltpu.VMEM((OCC, 8 * DEPTH), jnp.bfloat16),
            pltpu.VMEM((2, OCC, WIDTH), jnp.bfloat16),
            pltpu.SemaphoreType.DMA((IRREPS,)),
            pltpu.SemaphoreType.DMA((IRREPS,)),
            pltpu.SemaphoreType.DMA((IRREPS, D_KINDS)),
            pltpu.SemaphoreType.DMA((IRREPS, D_KINDS)),
            pltpu.SemaphoreType.DMA((PAIRS, A_KINDS)),
            pltpu.SemaphoreType.DMA((PAIRS, A_KINDS)),
            pltpu.SemaphoreType.DMA((8,)),
            pltpu.SemaphoreType.DMA((8,)),
            pltpu.SemaphoreType.DMA((2,)),
            pltpu.SemaphoreType.DMA((2,)),
        ],
        compiler_params=pltpu.CompilerParams(
            collective_id=0, has_side_effects=True, vmem_limit_bytes=52 << 20
        ),
        cost_estimate=pl.CostEstimate(flops=17 << 30, bytes_accessed=12 << 20, transcendentals=0),
    )(cd_count, ab_count, pairs, integrals)
    return ladder.transpose(1, 0, 2)


def solution(mesh):
    in_specs = (P("col", None, "row"), P(None, "col", "row"), P(), P())
    out_specs = P("col", None, "row")
    return jax.shard_map(
        per_device, mesh=mesh, in_specs=in_specs, out_specs=out_specs, check_vma=False
    )
```

```python
import functools

import jax
import jax.numpy as jnp
from jax import lax
from jax.experimental import pallas as pl
from jax.experimental.pallas import tpu as pltpu
from jax.sharding import PartitionSpec as P

MESH = pl.DeviceIdType.MESH
IRREPS = 8
PAIRS = 4
SIDE = 4
OCC = 512
DEPTH = 128
WIDTH = 1024
NABG = 8192
TILE = 256
D_KINDS = 10
A_KINDS = 20
UNITS = 36
STRIPS = 4
SLAB = 32
GROUP = 2 * DEPTH

PLAN = {
    0: [
        ("own_x", 1), ("own_x", 2), ("send_b", 1), ("on_x", 0, 4), ("on_x", 0, 5),
        ("form", 0, 0), ("on_x", 1, 4), ("on_x", 1, 5), ("form", 0, 1), ("own_x", 3),
        ("own_y", 1), ("up_y", 0), ("down_y", 0), ("on_x", 2, 4), ("on_x", 2, 5),
        ("up_z", 0), ("send_b", 2), ("form", 1, 0), ("share_up", 0), ("down_z", 0),
        ("share_down", 0), ("on_x", 3, 4), ("on_x", 3, 5), ("form", 1, 1), ("up_y", 1),
        ("down_y", 1), ("on_x", 0, 8), ("on_x", 0, 9), ("up_z", 1), ("far_y", 0),
        ("send_b", 3), ("on_x", 0, 12), ("on_x", 0, 13), ("share_up", 1), ("share_far", 0),
        ("form", 2, 0), ("down_z", 1), ("share_down", 1), ("own_y", 2), ("form", 2, 1),
        ("far_y", 1), ("on_x", 1, 8), ("on_x", 1, 9), ("send_b", 4), ("up_z", 2),
        ("on_x", 1, 12), ("on_x", 1, 13), ("form", 3, 0), ("share_up", 2), ("share_far", 1),
        ("form", 3, 1), ("on_x", 0, 16), ("on_x", 0, 17), ("send_b", 5), ("down_z", 2),
        ("share_down", 2), ("up_y", 2), ("down_y", 2), ("up_z", 3), ("on_x", 1, 16),
        ("on_x", 1, 17), ("form", 4, 0), ("share_up", 3), ("down_z", 3), ("share_down", 3),
        ("own_y", 3), ("form", 4, 1),
    ],
    1: [
        ("share_far", 2),
    ],
    2: [
        ("form", 5, 0), ("on_x", 2, 8), ("on_x", 2, 9), ("send_b", 6),
    ],
    3: [
        ("up_z", 4),
    ],
    4: [
        ("form", 5, 1), ("far_y", 2), ("on_x", 2, 12), ("on_x", 2, 13),
    ],
    5: [
        ("share_up", 4), ("share_far", 3), ("send_b", 7),
    ],
    6: [
        ("up_y", 3), ("down_y", 3), ("up_z", 5), ("down_z", 4), ("share_down", 4),
    ],
    8: [
        ("on_x", 2, 16), ("on_x", 2, 17),
    ],
    9: [
        ("form", 6, 0),
    ],
    11: [
        ("form", 6, 1), ("share_up", 5), ("down_z", 5), ("share_down", 5), ("on_x", 3, 8),
        ("on_x", 3, 9),
    ],
    13: [
        ("form", 7, 0), ("share_far", 4), ("on_x", 3, 12), ("on_x", 3, 13),
    ],
    14: [
        ("form", 7, 1), ("up_z", 6),
    ],
    15: [
        ("far_y", 3),
    ],
    17: [
        ("share_up", 6), ("down_z", 6), ("share_down", 6),
    ],
    19: [
        ("up_z", 7), ("share_far", 5),
    ],
    20: [
        ("on_x", 3, 16), ("on_x", 3, 17), ("share_up", 7),
    ],
    22: [
        ("down_z", 7), ("share_down", 7),
    ],
    24: [
        ("share_far", 6),
    ],
    25: [
        ("share_far", 7),
    ],
}


def ring(value, step):
    return lax.rem(value + step + SIDE, SIDE)


def kernel(
    cd_hbm, ab_hbm, amps_ref, ints_ref, out_ref,
    cd_ref, ab_ref, a_mine, a_all, b_mine, b_other, d_all, peaks, peaks_other, rows_up, scales, a_now, partial, staged,
    b_send, b_recv, d_send, d_recv, a_send, a_recv, s_send, s_recv, here_sem, out_sem,
):
    row, col = lax.axis_index("row"), lax.axis_index("col")
    y, x = row // SIDE, lax.rem(row, SIDE)
    z, core = col // 2, lax.rem(col, 2)
    other = 1 - core
    ids = lambda yy, xx, zz, cc: (yy * SIDE + xx, zz * 2 + cc)
    across = ids(ring(y, 2), x, z, core)
    up_y, down_y = ids(ring(y, 1), x, z, core), ids(ring(y, -1), x, z, core)
    up_x, down_x = ids(y, ring(x, 1), z, core), ids(y, ring(x, -1), z, core)
    up_z, down_z = ids(y, x, ring(z, 1), core), ids(y, x, ring(z, -1), core)
    sibling = ids(y, x, z, other)
    everyone_z = [ids(y, x, ring(z, s), core) for s in (1, 2, 3)]
    everyone_z += [ids(y, x, ring(z, s), other) for s in (0, 1, 2, 3)]
    near = [across, up_y, down_y, up_x, down_x, *everyone_z]

    barrier = pltpu.get_barrier_semaphore()
    for device in near:
        pl.semaphore_signal(barrier, inc=1, device_id=device, device_id_type=MESH)
    loads = [
        pltpu.make_async_copy(source, target, here_sem.at[n])
        for n, (source, target) in enumerate(
            ((amps_ref, a_mine), (ab_hbm, ab_ref), (cd_hbm, cd_ref), (ints_ref, b_mine))
        )
    ]
    for load in loads:
        load.start()

    def remote(source, target, send, recv, device):
        return pltpu.make_async_remote_copy(
            src_ref=source, dst_ref=target, send_sem=send, recv_sem=recv, device_id=device, device_id_type=MESH
        )

    low, high, whole = pl.ds(0, DEPTH // 2), pl.ds(DEPTH // 2, DEPTH // 2), pl.ds(0, DEPTH)
    halves = (low, high)

    def b_copy(g, h):
        return remote(
            ints_ref.at[g, halves[h]], b_other.at[g, halves[h]], b_send.at[g, h], b_recv.at[g, h], across
        )

    slot = lambda s, c: ring(z, s) * 2 + c
    d_kinds = [
        (slot(0, core), low, up_z, slot(-1, core)),
        (slot(0, core), high, up_z, slot(-1, core)),
        (slot(0, core), low, down_z, slot(1, core)),
        (slot(0, core), high, down_z, slot(1, core)),
        (slot(-1, core), low, up_z, slot(2, core)),
        (slot(1, core), high, down_z, slot(2, core)),
        (slot(0, core), whole, sibling, slot(0, other)),
        (slot(-1, core), whole, sibling, slot(-1, other)),
        (slot(1, core), whole, sibling, slot(1, other)),
        (slot(2, core), whole, sibling, slot(2, other)),
    ]

    def d_copy(g, kind, arriving=False):
        leaves, rows, device, fills = d_kinds[kind]
        place = d_all.at[g, fills if arriving else leaves, rows]
        return remote(place, place, d_send.at[g, kind], d_recv.at[g, kind], device)

    first, second, every = pl.ds(0, OCC // 2), pl.ds(OCC // 2, OCC // 2), pl.ds(0, OCC)
    block = lambda sy, sx: ring(y, sy) * SIDE + ring(x, sx)
    a_kinds = [
        (block(0, 0), every, up_y, block(-1, 0)),
        (block(0, 0), every, down_y, block(1, 0)),
        (block(-1, 0), first, up_y, block(2, 0)),
        (block(1, 0), second, down_y, block(2, 0)),
    ]
    for sy in (0, -1, 1, 2):
        a_kinds += [
            (block(sy, 0), every, up_x, block(sy, -1)),
            (block(sy, 0), every, down_x, block(sy, 1)),
            (block(sy, -1), first, up_x, block(sy, 2)),
            (block(sy, 1), second, down_x, block(sy, 2)),
        ]

    def a_copy(p, kind, arriving=False):
        leaves, rows, device, fills = a_kinds[kind]
        place = a_all.at[p, fills if arriving else leaves, rows]
        return remote(place, place, a_send.at[p, kind], a_recv.at[p, kind], device)

    def s_copy(n, mine):
        return remote(scales.at[mine], scales.at[mine], s_send.at[n], s_recv.at[n], everyone_z[n])

    def send_b(g):
        b_copy(g, 0).start()
        b_copy(g, 1).start()

    def moves(p, waits, starts):
        for kind in waits:
            a_copy(p, kind, True).wait_recv()
        for kind in starts:
            a_copy(p, kind).start()

    def passes(g, waits, kind):
        for arrived in waits:
            d_copy(g, arrived, True).wait_recv()
        d_copy(g, kind).start()

    lane = lax.broadcasted_iota(jnp.int32, (DEPTH // 2, DEPTH), 1)
    depth_at = col * DEPTH + lax.broadcasted_iota(jnp.int32, (DEPTH // 2, WIDTH), 0)
    place_at = lax.rem(row, SIDE * SIDE // 2) * WIDTH + lax.broadcasted_iota(jnp.int32, (DEPTH // 2, WIDTH), 1)

    def form(g, h):
        ups = jnp.sum(jnp.where(lane == g, rows_up[halves[h], :], 0.0), axis=1, keepdims=True) * 32768.0
        b_copy(g, h).wait_recv()
        mine, theirs = b_mine[g, halves[h], :], b_other[g, halves[h], :]
        difference = mine.astype(jnp.float32) - theirs.astype(jnp.float32)
        keep = (depth_at < cd_ref[g] - h * (DEPTH // 2)) & (place_at < ab_ref[g])
        scaled = jnp.where(keep, difference * ups, 0.0)
        whole_number = jnp.round(jnp.minimum(scaled, 32767.0)).astype(jnp.int32)
        d_all[g, col, halves[h], :] = whole_number.astype(jnp.int16)
        d_copy(g, h).start()
        d_copy(g, 2 + h).start()
        if h == 1:
            d_copy(g, 6).start()

    does = {
        "form": form,
        "send_b": send_b,
        "own_x": lambda p: moves(p, (), (4, 5)),
        "own_y": lambda p: moves(p, (), (0, 1)),
        "up_y": lambda p: moves(p, (0,), (2, 8, 9)),
        "down_y": lambda p: moves(p, (1,), (3, 12, 13)),
        "far_y": lambda p: moves(p, (2, 3), (16, 17)),
        "on_x": lambda p, kind: moves(p, (kind,), (kind + 2,)),
        "up_z": lambda g: passes(g, (0,), 4),
        "down_z": lambda g: passes(g, (3,), 5),
        "share_up": lambda g: passes(g, (1,), 7),
        "share_down": lambda g: passes(g, (2,), 8),
        "share_far": lambda g: passes(g, (4, 5), 9),
    }

    half = lax.broadcasted_iota(jnp.int32, (OCC, DEPTH), 1) < DEPTH // 2
    chips = (0, -1, 1, 2)

    def product(g, groups, at):
        d = jnp.concatenate(
            [d_all[g, pl.ds(2 * ring(z, chips[i]), 2), :, at].reshape(GROUP, TILE) for i in groups], axis=0
        ).astype(jnp.float32)
        top = d.astype(jnp.bfloat16)
        rest = (d - top.astype(jnp.float32)).astype(jnp.bfloat16)
        a = a_now[:, groups[0] * GROUP : (groups[-1] + 1) * GROUP]
        summed = jnp.dot(a, top, preferred_element_type=jnp.float32)
        summed += jnp.dot(a, rest, preferred_element_type=jnp.float32)
        return summed * (1.0 / 32768.0)

    def gather(g):
        p, parity = g // 2, lax.rem(g, 2)

        @pl.when(parity == 0)
        def _():
            for kind in (6, 7, 10, 11, 14, 15, 18, 19):
                a_copy(p, kind, True).wait_recv()

        for kind in (6, 7, 8):
            d_copy(g, kind, True).wait_recv()
        for i in range(SIDE):
            for c in (0, 1):
                m = 2 * ring(z, chips[i]) + c
                left = pltpu.roll(a_all[p, 2 * m].astype(jnp.float32), 64 * parity, 1)
                right = pltpu.roll(a_all[p, 2 * m + 1].astype(jnp.float32), 64 - 64 * parity, 1)
                joined = jnp.where(half, left, right) * scales[m, pl.ds(g, 1), :]
                k = (2 * i + c) * DEPTH
                a_now[:, k : k + DEPTH] = joined.astype(jnp.bfloat16)

    def strip(n):
        return pl.ds(pl.multiple_of(n * TILE, TILE), TILE)

    def out_copy(g, n):
        parity = lax.rem(g, 2)
        return pltpu.make_async_copy(
            staged.at[parity, n], out_ref.at[g, :, strip(n)], out_sem.at[parity, n]
        )

    def multiply_most(g, n):
        partial[n] = product(g, (0, 1, 2), strip(n))

    def multiply_rest(g, n):
        pl.when(g >= 2)(lambda: out_copy(g - 2, n).wait())
        staged[lax.rem(g, 2), n] = (partial[n] + product(g, (3,), strip(n))).astype(jnp.bfloat16)
        out_copy(g, n).start()

    for load in loads[1:]:
        load.wait()

    def peak(g, _):
        most = []
        for h in (0, 1):
            size = jnp.abs(b_mine[g, halves[h], :].astype(jnp.float32))
            size = jnp.where(place_at < ab_ref[g], size, 0.0)
            most.append(jnp.max(size, axis=1, keepdims=True))
        spread = jnp.broadcast_to(jnp.concatenate(most, axis=0), (DEPTH, DEPTH))
        peaks[pl.ds(g, 1), :] = jnp.transpose(spread)[0:1, :]
        return 0

    lax.fori_loop(0, IRREPS, peak, 0)
    pl.semaphore_wait(barrier, len(near))
    peak_copy = remote(peaks, peaks_other, s_send.at[7], s_recv.at[7], across)
    peak_copy.start()
    send_b(0)
    loads[0].wait()
    for p in range(PAIRS):
        a_all[p, row] = jnp.transpose(a_mine[p].astype(jnp.float32)).astype(jnp.bfloat16)
        if p == 0:
            moves(0, (), (4, 5, 0, 1))
    peak_copy.wait_recv()
    left = peaks[...] + peaks_other[...]
    up, down = jnp.ones_like(left), jnp.ones_like(left)
    for power in (32, 16, 8, 4, 2, 1):
        small = left < 2.0**-power
        left = jnp.where(small, left * 2.0**power, left)
        up = jnp.where(small, up * 2.0**power, up)
        down = jnp.where(small, down * 2.0**-power, down)
    rows_up[...] = jnp.transpose(jnp.concatenate([up] * 16, axis=0))
    scales[col] = down
    for n in range(7):
        s_copy(n, col).start()

    def unit(i, _):
        for at, calls in PLAN.items():
            @pl.when(i == at)
            def _(calls=calls):
                for name, *where in calls:
                    does[name](*where)

        @pl.when(i == 0)
        def _():
            sender = [slot(-1, core), slot(-2, core), slot(-3, core)] + [slot(-n, other) for n in (0, 1, 2, 3)]
            for n in range(7):
                s_copy(n, sender[n]).wait_recv()

        g, n = i // STRIPS, lax.rem(i, STRIPS)
        last = IRREPS * STRIPS

        @pl.when(i < last)
        def _():
            pl.when(n == 0)(lambda: gather(g))
            multiply_most(g, n)

        @pl.when((i < last - STRIPS) | (i >= last))
        def _():
            block = g - i // last
            pl.when(n == 0)(lambda: d_copy(block, 9, True).wait_recv())
            multiply_rest(block, n)

        return 0

    lax.fori_loop(0, UNITS, unit, 0)

    for n in range(7):
        s_copy(n, col).wait_send()
    peak_copy.wait_send()

    def drain_b(g, _):
        b_copy(g, 0).wait_send()
        b_copy(g, 1).wait_send()
        for kind in range(D_KINDS):
            d_copy(g, kind).wait_send()
        return 0

    def drain_a(p, _):
        for kind in range(A_KINDS):
            a_copy(p, kind).wait_send()
        return 0

    lax.fori_loop(0, IRREPS, drain_b, 0)
    lax.fori_loop(0, PAIRS, drain_a, 0)
    for n in range(STRIPS):
        out_copy(IRREPS - 2, n).wait()
        out_copy(IRREPS - 1, n).wait()


def interleave(in_ref, out_ref, taken, given, in_sem, out_sem):
    def take(n):
        return pltpu.make_async_copy(in_ref.at[:, pl.ds(n * SLAB, SLAB), :], taken.at[n], in_sem.at[n])

    def give(n):
        rows = pl.ds(pl.multiple_of(n * (SLAB * IRREPS), SLAB * IRREPS), SLAB * IRREPS)
        return pltpu.make_async_copy(given.at[n], out_ref.at[rows], out_sem.at[n])

    slabs = OCC // SLAB
    for n in range(slabs):
        take(n).start()

    def slab(n, _):
        take(n).wait()
        given[n] = jnp.swapaxes(taken[n], 0, 1).reshape(SLAB * IRREPS, WIDTH)
        give(n).start()
        return 0

    lax.fori_loop(0, slabs, slab, 0)
    for n in range(slabs):
        give(n).wait()


def per_device(amplitudes, integrals, cd_count, ab_count):
    pairs = amplitudes.transpose(1, 2, 0).reshape(PAIRS, DEPTH, OCC)
    by_irrep = pl.pallas_call(
        kernel,
        out_shape=jax.ShapeDtypeStruct((IRREPS, OCC, WIDTH), jnp.bfloat16),
        in_specs=[pl.BlockSpec(memory_space=pl.ANY)] * 4,
        out_specs=pl.BlockSpec(memory_space=pl.ANY),
        scratch_shapes=[
            pltpu.SMEM((IRREPS,), jnp.int32),
            pltpu.SMEM((IRREPS,), jnp.int32),
            pltpu.VMEM((PAIRS, DEPTH, OCC), jnp.bfloat16),
            pltpu.VMEM((PAIRS, 16, OCC, DEPTH), jnp.bfloat16),
            pltpu.VMEM((IRREPS, DEPTH, WIDTH), jnp.bfloat16),
            pltpu.VMEM((IRREPS, DEPTH, WIDTH), jnp.bfloat16),
            pltpu.VMEM((IRREPS, 8, DEPTH, WIDTH), jnp.int16),
            pltpu.VMEM((IRREPS, DEPTH), jnp.float32),
            pltpu.VMEM((IRREPS, DEPTH), jnp.float32),
            pltpu.VMEM((DEPTH, DEPTH), jnp.float32),
            pltpu.VMEM((8, IRREPS, DEPTH), jnp.float32),
            pltpu.VMEM((OCC, 8 * DEPTH), jnp.bfloat16),
            pltpu.VMEM((STRIPS, OCC, TILE), jnp.float32),
            pltpu.VMEM((2, STRIPS, OCC, TILE), jnp.bfloat16),
            pltpu.SemaphoreType.DMA((IRREPS, 2)),
            pltpu.SemaphoreType.DMA((IRREPS, 2)),
            pltpu.SemaphoreType.DMA((IRREPS, D_KINDS)),
            pltpu.SemaphoreType.DMA((IRREPS, D_KINDS)),
            pltpu.SemaphoreType.DMA((PAIRS, A_KINDS)),
            pltpu.SemaphoreType.DMA((PAIRS, A_KINDS)),
            pltpu.SemaphoreType.DMA((8,)),
            pltpu.SemaphoreType.DMA((8,)),
            pltpu.SemaphoreType.DMA((4,)),
            pltpu.SemaphoreType.DMA((2, STRIPS)),
        ],
        compiler_params=pltpu.CompilerParams(
            collective_id=0, has_side_effects=True, vmem_limit_bytes=60 << 20
        ),
        cost_estimate=pl.CostEstimate(flops=17 << 30, bytes_accessed=12 << 20, transcendentals=0),
    )(cd_count, ab_count, pairs, integrals)
    slabs = OCC // SLAB
    ladder = pl.pallas_call(
        interleave,
        out_shape=jax.ShapeDtypeStruct((OCC * IRREPS, WIDTH), jnp.bfloat16),
        in_specs=[pl.BlockSpec(memory_space=pl.ANY)],
        out_specs=pl.BlockSpec(memory_space=pl.ANY),
        scratch_shapes=[
            pltpu.VMEM((slabs, IRREPS, SLAB, WIDTH), jnp.bfloat16),
            pltpu.VMEM((slabs, SLAB * IRREPS, WIDTH), jnp.bfloat16),
            pltpu.SemaphoreType.DMA((slabs,)),
            pltpu.SemaphoreType.DMA((slabs,)),
        ],
        compiler_params=pltpu.CompilerParams(vmem_limit_bytes=60 << 20),
    )(by_irrep)
    return ladder.reshape(OCC, IRREPS, WIDTH)


def solution(mesh):
    in_specs = (P("col", None, "row"), P(None, "col", "row"), P(), P())
    out_specs = P("col", None, "row")
    return jax.shard_map(
        per_device, mesh=mesh, in_specs=in_specs, out_specs=out_specs, check_vma=False
    )
```

```python
import functools

import jax
import jax.numpy as jnp
from jax import lax
from jax.experimental import pallas as pl
from jax.experimental.pallas import tpu as pltpu
from jax.sharding import PartitionSpec as P

MESH = pl.DeviceIdType.MESH
IRREPS = 8
PAIRS = 4
SIDE = 4
OCC = 512
DEPTH = 128
WIDTH = 1024
NABG = 8192
TILE = 1024
D_KINDS = 10
A_KINDS = 20
UNITS = 9
STRIPS = 1
SLAB = 32
GROUP = 2 * DEPTH

PLAN = {
    0: [
        ("own_x", 1), ("send_b", 1), ("own_x", 2), ("on_x", 0, 4), ("on_x", 0, 5),
        ("form", 0, 0), ("on_x", 1, 4), ("on_x", 1, 5), ("send_b", 2), ("form", 0, 1),
        ("own_x", 3), ("up_y", 0), ("down_y", 0), ("on_x", 2, 4), ("on_x", 2, 5),
        ("up_z", 0), ("form", 1, 0), ("share_up", 0), ("down_z", 0), ("share_down", 0),
        ("own_y", 1), ("on_x", 3, 4), ("on_x", 3, 5), ("form", 1, 1), ("send_b", 3),
        ("on_x", 0, 8), ("on_x", 0, 9), ("form", 2, 0), ("up_z", 1), ("on_x", 0, 12),
        ("on_x", 0, 13), ("form", 2, 1), ("share_far", 0), ("share_up", 1), ("far_y", 0),
        ("send_b", 4), ("down_z", 1), ("share_down", 1), ("up_z", 2), ("up_y", 1),
        ("down_y", 1), ("form", 3, 0), ("on_x", 0, 16), ("on_x", 0, 17), ("own_y", 2),
        ("down_z", 2), ("share_down", 2), ("share_up", 2), ("form", 3, 1), ("on_x", 1, 8),
        ("on_x", 1, 9), ("send_b", 5), ("share_far", 1), ("form", 4, 0), ("on_x", 1, 12),
        ("on_x", 1, 13), ("up_z", 3),
    ],
    1: [
        ("form", 4, 1), ("far_y", 1), ("share_far", 2), ("share_up", 3), ("up_y", 2),
        ("down_y", 2), ("down_z", 3), ("share_down", 3), ("up_z", 4), ("send_b", 6),
    ],
    2: [
        ("form", 5, 0), ("own_y", 3), ("on_x", 1, 16), ("on_x", 1, 17), ("form", 5, 1),
        ("down_z", 4), ("share_down", 4), ("share_up", 4), ("far_y", 2), ("send_b", 7),
        ("on_x", 2, 8), ("on_x", 2, 9), ("share_far", 3), ("form", 6, 0), ("on_x", 2, 12),
        ("on_x", 2, 13), ("up_z", 5),
    ],
    3: [
        ("form", 6, 1), ("down_z", 5), ("share_down", 5), ("share_up", 5), ("on_x", 2, 16),
        ("on_x", 2, 17), ("up_y", 3), ("down_y", 3),
    ],
    4: [
        ("share_far", 4), ("up_z", 6), ("form", 7, 0), ("form", 7, 1), ("far_y", 3),
        ("down_z", 6), ("share_down", 6), ("share_up", 6), ("on_x", 3, 8), ("on_x", 3, 9),
    ],
    5: [
        ("share_far", 5), ("on_x", 3, 12), ("on_x", 3, 13), ("up_z", 7), ("on_x", 3, 16),
        ("on_x", 3, 17),
    ],
    6: [
        ("down_z", 7), ("share_down", 7), ("share_up", 7), ("share_far", 6),
    ],
    7: [
        ("share_far", 7),
    ],
}


def ring(value, step):
    return lax.rem(value + step + SIDE, SIDE)


def kernel(
    cd_hbm, ab_hbm, amps_ref, ints_ref, out_ref,
    cd_ref, ab_ref, a_mine, a_all, b_mine, b_other, d_all, peaks, peaks_other, rows_up, scales, a_now, partial, staged,
    b_send, b_recv, d_send, d_recv, a_send, a_recv, s_send, s_recv, here_sem, out_sem,
):
    row, col = lax.axis_index("row"), lax.axis_index("col")
    y, x = row // SIDE, lax.rem(row, SIDE)
    z, core = col // 2, lax.rem(col, 2)
    other = 1 - core
    ids = lambda yy, xx, zz, cc: (yy * SIDE + xx, zz * 2 + cc)
    across = ids(ring(y, 2), x, z, core)
    up_y, down_y = ids(ring(y, 1), x, z, core), ids(ring(y, -1), x, z, core)
    up_x, down_x = ids(y, ring(x, 1), z, core), ids(y, ring(x, -1), z, core)
    up_z, down_z = ids(y, x, ring(z, 1), core), ids(y, x, ring(z, -1), core)
    sibling = ids(y, x, z, other)
    everyone_z = [ids(y, x, ring(z, s), core) for s in (1, 2, 3)]
    everyone_z += [ids(y, x, ring(z, s), other) for s in (0, 1, 2, 3)]
    near = [across, up_y, down_y, up_x, down_x, *everyone_z]

    barrier = pltpu.get_barrier_semaphore()
    for device in near:
        pl.semaphore_signal(barrier, inc=1, device_id=device, device_id_type=MESH)
    loads = [
        pltpu.make_async_copy(source, target, here_sem.at[n])
        for n, (source, target) in enumerate(
            ((amps_ref, a_mine), (ab_hbm, ab_ref), (cd_hbm, cd_ref), (ints_ref, b_mine))
        )
    ]
    for load in loads:
        load.start()

    def remote(source, target, send, recv, device):
        return pltpu.make_async_remote_copy(
            src_ref=source, dst_ref=target, send_sem=send, recv_sem=recv, device_id=device, device_id_type=MESH
        )

    low, high, whole = pl.ds(0, DEPTH // 2), pl.ds(DEPTH // 2, DEPTH // 2), pl.ds(0, DEPTH)
    halves = (low, high)

    def b_copy(g, h):
        return remote(
            ints_ref.at[g, halves[h]], b_other.at[g, halves[h]], b_send.at[g, h], b_recv.at[g, h], across
        )

    slot = lambda s, c: ring(z, s) * 2 + c
    d_kinds = [
        (slot(0, core), low, up_z, slot(-1, core)),
        (slot(0, core), high, up_z, slot(-1, core)),
        (slot(0, core), low, down_z, slot(1, core)),
        (slot(0, core), high, down_z, slot(1, core)),
        (slot(-1, core), low, up_z, slot(2, core)),
        (slot(1, core), high, down_z, slot(2, core)),
        (slot(0, core), whole, sibling, slot(0, other)),
        (slot(-1, core), whole, sibling, slot(-1, other)),
        (slot(1, core), whole, sibling, slot(1, other)),
        (slot(2, core), whole, sibling, slot(2, other)),
    ]

    def d_copy(g, kind, arriving=False):
        leaves, rows, device, fills = d_kinds[kind]
        place = d_all.at[g, fills if arriving else leaves, rows]
        return remote(place, place, d_send.at[g, kind], d_recv.at[g, kind], device)

    first, second, every = pl.ds(0, OCC // 2), pl.ds(OCC // 2, OCC // 2), pl.ds(0, OCC)
    block = lambda sy, sx: ring(y, sy) * SIDE + ring(x, sx)
    a_kinds = [
        (block(0, 0), every, up_y, block(-1, 0)),
        (block(0, 0), every, down_y, block(1, 0)),
        (block(-1, 0), first, up_y, block(2, 0)),
        (block(1, 0), second, down_y, block(2, 0)),
    ]
    for sy in (0, -1, 1, 2):
        a_kinds += [
            (block(sy, 0), every, up_x, block(sy, -1)),
            (block(sy, 0), every, down_x, block(sy, 1)),
            (block(sy, -1), first, up_x, block(sy, 2)),
            (block(sy, 1), second, down_x, block(sy, 2)),
        ]

    def a_copy(p, kind, arriving=False):
        leaves, rows, device, fills = a_kinds[kind]
        place = a_all.at[p, fills if arriving else leaves, rows]
        return remote(place, place, a_send.at[p, kind], a_recv.at[p, kind], device)

    def s_copy(n, mine):
        return remote(scales.at[mine], scales.at[mine], s_send.at[n], s_recv.at[n], everyone_z[n])

    def send_b(g):
        b_copy(g, 0).start()
        b_copy(g, 1).start()

    def moves(p, waits, starts):
        for kind in waits:
            a_copy(p, kind, True).wait_recv()
        for kind in starts:
            a_copy(p, kind).start()

    def passes(g, waits, kind):
        for arrived in waits:
            d_copy(g, arrived, True).wait_recv()
        d_copy(g, kind).start()

    lane = lax.broadcasted_iota(jnp.int32, (DEPTH // 2, DEPTH), 1)
    depth_at = col * DEPTH + lax.broadcasted_iota(jnp.int32, (DEPTH // 2, WIDTH), 0)
    place_at = lax.rem(row, SIDE * SIDE // 2) * WIDTH + lax.broadcasted_iota(jnp.int32, (DEPTH // 2, WIDTH), 1)

    def form(g, h):
        ups = jnp.sum(jnp.where(lane == g, rows_up[halves[h], :], 0.0), axis=1, keepdims=True) * 32768.0
        b_copy(g, h).wait_recv()
        mine, theirs = b_mine[g, halves[h], :], b_other[g, halves[h], :]
        difference = mine.astype(jnp.float32) - theirs.astype(jnp.float32)
        keep = (depth_at < cd_ref[g] - h * (DEPTH // 2)) & (place_at < ab_ref[g])
        scaled = jnp.where(keep, difference * ups, 0.0)
        whole_number = jnp.round(jnp.minimum(scaled, 32767.0)).astype(jnp.int32)
        d_all[g, col, halves[h], :] = whole_number.astype(jnp.int16)
        d_copy(g, h).start()
        d_copy(g, 2 + h).start()
        if h == 1:
            d_copy(g, 6).start()

    does = {
        "form": form,
        "send_b": send_b,
        "own_x": lambda p: moves(p, (), (4, 5)),
        "own_y": lambda p: moves(p, (), (0, 1)),
        "up_y": lambda p: moves(p, (0,), (2, 8, 9)),
        "down_y": lambda p: moves(p, (1,), (3, 12, 13)),
        "far_y": lambda p: moves(p, (2, 3), (16, 17)),
        "on_x": lambda p, kind: moves(p, (kind,), (kind + 2,)),
        "up_z": lambda g: passes(g, (0,), 4),
        "down_z": lambda g: passes(g, (3,), 5),
        "share_up": lambda g: passes(g, (1,), 7),
        "share_down": lambda g: passes(g, (2,), 8),
        "share_far": lambda g: passes(g, (4, 5), 9),
    }

    half = lax.broadcasted_iota(jnp.int32, (OCC, DEPTH), 1) < DEPTH // 2
    chips = (0, -1, 1, 2)

    def product(g, groups, at):
        d = jnp.concatenate(
            [d_all[g, pl.ds(2 * ring(z, chips[i]), 2), :, at].reshape(GROUP, TILE) for i in groups], axis=0
        ).astype(jnp.float32)
        top = d.astype(jnp.bfloat16)
        rest = (d - top.astype(jnp.float32)).astype(jnp.bfloat16)
        a = a_now[:, groups[0] * GROUP : (groups[-1] + 1) * GROUP]
        summed = jnp.dot(a, top, preferred_element_type=jnp.float32)
        summed += jnp.dot(a, rest, preferred_element_type=jnp.float32)
        return summed * (1.0 / 32768.0)

    def gather(g):
        p, parity = g // 2, lax.rem(g, 2)

        @pl.when(parity == 0)
        def _():
            for kind in (6, 7, 10, 11, 14, 15, 18, 19):
                a_copy(p, kind, True).wait_recv()

        for kind in (6, 7, 8):
            d_copy(g, kind, True).wait_recv()
        for i in range(SIDE):
            for c in (0, 1):
                m = 2 * ring(z, chips[i]) + c
                left = pltpu.roll(a_all[p, 2 * m].astype(jnp.float32), 64 * parity, 1)
                right = pltpu.roll(a_all[p, 2 * m + 1].astype(jnp.float32), 64 - 64 * parity, 1)
                joined = jnp.where(half, left, right) * scales[m, pl.ds(g, 1), :]
                k = (2 * i + c) * DEPTH
                a_now[:, k : k + DEPTH] = joined.astype(jnp.bfloat16)

    def strip(n):
        return pl.ds(pl.multiple_of(n * TILE, TILE), TILE)

    def out_copy(g, n):
        parity = lax.rem(g, 2)
        return pltpu.make_async_copy(
            staged.at[parity, n], out_ref.at[g, :, strip(n)], out_sem.at[parity, n]
        )

    def multiply_most(g, n):
        partial[n] = product(g, (0, 1, 2), strip(n))

    def multiply_rest(g, n):
        pl.when(g >= 2)(lambda: out_copy(g - 2, n).wait())
        staged[lax.rem(g, 2), n] = (partial[n] + product(g, (3,), strip(n))).astype(jnp.bfloat16)
        out_copy(g, n).start()

    for load in loads[1:]:
        load.wait()

    def peak(g, _):
        most = []
        for h in (0, 1):
            size = jnp.abs(b_mine[g, halves[h], :].astype(jnp.float32))
            size = jnp.where(place_at < ab_ref[g], size, 0.0)
            most.append(jnp.max(size, axis=1, keepdims=True))
        spread = jnp.broadcast_to(jnp.concatenate(most, axis=0), (DEPTH, DEPTH))
        peaks[pl.ds(g, 1), :] = jnp.transpose(spread)[0:1, :]
        return 0

    lax.fori_loop(0, IRREPS, peak, 0)
    pl.semaphore_wait(barrier, len(near))
    peak_copy = remote(peaks, peaks_other, s_send.at[7], s_recv.at[7], across)
    peak_copy.start()
    send_b(0)
    loads[0].wait()
    for p in range(PAIRS):
        a_all[p, row] = jnp.transpose(a_mine[p].astype(jnp.float32)).astype(jnp.bfloat16)
        if p == 0:
            moves(0, (), (4, 5, 0, 1))
    peak_copy.wait_recv()
    left = peaks[...] + peaks_other[...]
    up, down = jnp.ones_like(left), jnp.ones_like(left)
    for power in (32, 16, 8, 4, 2, 1):
        small = left < 2.0**-power
        left = jnp.where(small, left * 2.0**power, left)
        up = jnp.where(small, up * 2.0**power, up)
        down = jnp.where(small, down * 2.0**-power, down)
    rows_up[...] = jnp.transpose(jnp.concatenate([up] * 16, axis=0))
    scales[col] = down
    for n in range(7):
        s_copy(n, col).start()

    def unit(i, _):
        for at, calls in PLAN.items():
            @pl.when(i == at)
            def _(calls=calls):
                for name, *where in calls:
                    does[name](*where)

        @pl.when(i == 0)
        def _():
            sender = [slot(-1, core), slot(-2, core), slot(-3, core)] + [slot(-n, other) for n in (0, 1, 2, 3)]
            for n in range(7):
                s_copy(n, sender[n]).wait_recv()

        g, n = i // STRIPS, lax.rem(i, STRIPS)
        last = IRREPS * STRIPS

        @pl.when(i < last)
        def _():
            pl.when(n == 0)(lambda: gather(g))
            multiply_most(g, n)

        @pl.when((i < last - STRIPS) | (i >= last))
        def _():
            block = g - i // last
            pl.when(n == 0)(lambda: d_copy(block, 9, True).wait_recv())
            multiply_rest(block, n)

        return 0

    lax.fori_loop(0, UNITS, unit, 0)

    for n in range(7):
        s_copy(n, col).wait_send()
    peak_copy.wait_send()

    def drain_b(g, _):
        b_copy(g, 0).wait_send()
        b_copy(g, 1).wait_send()
        for kind in range(D_KINDS):
            d_copy(g, kind).wait_send()
        return 0

    def drain_a(p, _):
        for kind in range(A_KINDS):
            a_copy(p, kind).wait_send()
        return 0

    lax.fori_loop(0, IRREPS, drain_b, 0)
    lax.fori_loop(0, PAIRS, drain_a, 0)
    for n in range(STRIPS):
        out_copy(IRREPS - 2, n).wait()
        out_copy(IRREPS - 1, n).wait()


def interleave(in_ref, out_ref, taken, given, in_sem, out_sem):
    def take(n):
        return pltpu.make_async_copy(in_ref.at[:, pl.ds(n * SLAB, SLAB), :], taken.at[n], in_sem.at[n])

    def give(n):
        rows = pl.ds(pl.multiple_of(n * (SLAB * IRREPS), SLAB * IRREPS), SLAB * IRREPS)
        return pltpu.make_async_copy(given.at[n], out_ref.at[rows], out_sem.at[n])

    slabs = OCC // SLAB
    for n in range(slabs):
        take(n).start()

    def slab(n, _):
        take(n).wait()
        given[n] = jnp.swapaxes(taken[n], 0, 1).reshape(SLAB * IRREPS, WIDTH)
        give(n).start()
        return 0

    lax.fori_loop(0, slabs, slab, 0)
    for n in range(slabs):
        give(n).wait()


def per_device(amplitudes, integrals, cd_count, ab_count):
    pairs = amplitudes.transpose(1, 2, 0).reshape(PAIRS, DEPTH, OCC)
    by_irrep = pl.pallas_call(
        kernel,
        out_shape=jax.ShapeDtypeStruct((IRREPS, OCC, WIDTH), jnp.bfloat16),
        in_specs=[pl.BlockSpec(memory_space=pl.ANY)] * 4,
        out_specs=pl.BlockSpec(memory_space=pl.ANY),
        scratch_shapes=[
            pltpu.SMEM((IRREPS,), jnp.int32),
            pltpu.SMEM((IRREPS,), jnp.int32),
            pltpu.VMEM((PAIRS, DEPTH, OCC), jnp.bfloat16),
            pltpu.VMEM((PAIRS, 16, OCC, DEPTH), jnp.bfloat16),
            pltpu.VMEM((IRREPS, DEPTH, WIDTH), jnp.bfloat16),
            pltpu.VMEM((IRREPS, DEPTH, WIDTH), jnp.bfloat16),
            pltpu.VMEM((IRREPS, 8, DEPTH, WIDTH), jnp.int16),
            pltpu.VMEM((IRREPS, DEPTH), jnp.float32),
            pltpu.VMEM((IRREPS, DEPTH), jnp.float32),
            pltpu.VMEM((DEPTH, DEPTH), jnp.float32),
            pltpu.VMEM((8, IRREPS, DEPTH), jnp.float32),
            pltpu.VMEM((OCC, 8 * DEPTH), jnp.bfloat16),
            pltpu.VMEM((STRIPS, OCC, TILE), jnp.float32),
            pltpu.VMEM((2, STRIPS, OCC, TILE), jnp.bfloat16),
            pltpu.SemaphoreType.DMA((IRREPS, 2)),
            pltpu.SemaphoreType.DMA((IRREPS, 2)),
            pltpu.SemaphoreType.DMA((IRREPS, D_KINDS)),
            pltpu.SemaphoreType.DMA((IRREPS, D_KINDS)),
            pltpu.SemaphoreType.DMA((PAIRS, A_KINDS)),
            pltpu.SemaphoreType.DMA((PAIRS, A_KINDS)),
            pltpu.SemaphoreType.DMA((8,)),
            pltpu.SemaphoreType.DMA((8,)),
            pltpu.SemaphoreType.DMA((4,)),
            pltpu.SemaphoreType.DMA((2, STRIPS)),
        ],
        compiler_params=pltpu.CompilerParams(
            collective_id=0, has_side_effects=True, vmem_limit_bytes=60 << 20
        ),
        cost_estimate=pl.CostEstimate(flops=17 << 30, bytes_accessed=12 << 20, transcendentals=0),
    )(cd_count, ab_count, pairs, integrals)
    slabs = OCC // SLAB
    ladder = pl.pallas_call(
        interleave,
        out_shape=jax.ShapeDtypeStruct((OCC * IRREPS, WIDTH), jnp.bfloat16),
        in_specs=[pl.BlockSpec(memory_space=pl.ANY)],
        out_specs=pl.BlockSpec(memory_space=pl.ANY),
        scratch_shapes=[
            pltpu.VMEM((slabs, IRREPS, SLAB, WIDTH), jnp.bfloat16),
            pltpu.VMEM((slabs, SLAB * IRREPS, WIDTH), jnp.bfloat16),
            pltpu.SemaphoreType.DMA((slabs,)),
            pltpu.SemaphoreType.DMA((slabs,)),
        ],
        compiler_params=pltpu.CompilerParams(vmem_limit_bytes=60 << 20),
    )(by_irrep)
    return ladder.reshape(OCC, IRREPS, WIDTH)


def solution(mesh):
    in_specs = (P("col", None, "row"), P(None, "col", "row"), P(), P())
    out_specs = P("col", None, "row")
    return jax.shard_map(
        per_device, mesh=mesh, in_specs=in_specs, out_specs=out_specs, check_vma=False
    )
```

```python
import functools

import jax
import jax.numpy as jnp
from jax import lax
from jax.experimental import pallas as pl
from jax.experimental.pallas import tpu as pltpu
from jax.sharding import PartitionSpec as P

MESH = pl.DeviceIdType.MESH
IRREPS = 8
PAIRS = 4
SIDE = 4
OCC = 512
DEPTH = 128
WIDTH = 1024
NABG = 8192
TILE = 1024
D_KINDS = 10
A_KINDS = 20
UNITS = 9
STRIPS = 1
SLAB = 32
GROUP = 2 * DEPTH

PLAN = {
    0: [
        ("own_x", 1), ("send_b", 1), ("own_x", 2), ("on_x", 0, 4), ("on_x", 0, 5),
        ("form", 0, 0), ("on_x", 1, 4), ("on_x", 1, 5), ("send_b", 2), ("form", 0, 1),
        ("own_x", 3), ("up_y", 0), ("down_y", 0), ("on_x", 2, 4), ("on_x", 2, 5),
        ("up_z", 0), ("form", 1, 0), ("share_up", 0), ("down_z", 0), ("share_down", 0),
        ("own_y", 1), ("on_x", 3, 4), ("on_x", 3, 5), ("form", 1, 1), ("send_b", 3),
        ("on_x", 0, 8), ("on_x", 0, 9), ("form", 2, 0), ("up_z", 1), ("on_x", 0, 12),
        ("on_x", 0, 13), ("form", 2, 1), ("share_far", 0), ("share_up", 1), ("far_y", 0),
        ("send_b", 4), ("down_z", 1), ("share_down", 1), ("up_z", 2), ("up_y", 1),
        ("down_y", 1), ("form", 3, 0), ("on_x", 0, 16), ("on_x", 0, 17), ("own_y", 2),
        ("down_z", 2), ("share_down", 2), ("share_up", 2), ("form", 3, 1), ("on_x", 1, 8),
        ("on_x", 1, 9), ("send_b", 5), ("share_far", 1), ("form", 4, 0), ("on_x", 1, 12),
        ("on_x", 1, 13), ("up_z", 3),
    ],
    1: [
        ("form", 4, 1), ("far_y", 1), ("share_far", 2), ("share_up", 3), ("up_y", 2),
        ("down_y", 2), ("down_z", 3), ("share_down", 3), ("up_z", 4), ("send_b", 6),
    ],
    2: [
        ("form", 5, 0), ("own_y", 3), ("on_x", 1, 16), ("on_x", 1, 17), ("form", 5, 1),
        ("down_z", 4), ("share_down", 4), ("share_up", 4), ("far_y", 2), ("send_b", 7),
        ("on_x", 2, 8), ("on_x", 2, 9), ("share_far", 3), ("form", 6, 0), ("on_x", 2, 12),
        ("on_x", 2, 13), ("up_z", 5),
    ],
    3: [
        ("form", 6, 1), ("down_z", 5), ("share_down", 5), ("share_up", 5), ("on_x", 2, 16),
        ("on_x", 2, 17), ("up_y", 3), ("down_y", 3),
    ],
    4: [
        ("share_far", 4), ("up_z", 6), ("form", 7, 0), ("form", 7, 1), ("far_y", 3),
        ("down_z", 6), ("share_down", 6), ("share_up", 6), ("on_x", 3, 8), ("on_x", 3, 9),
    ],
    5: [
        ("share_far", 5), ("on_x", 3, 12), ("on_x", 3, 13), ("up_z", 7), ("on_x", 3, 16),
        ("on_x", 3, 17),
    ],
    6: [
        ("down_z", 7), ("share_down", 7), ("share_up", 7), ("share_far", 6),
    ],
    7: [
        ("share_far", 7),
    ],
}


def ring(value, step):
    return lax.rem(value + step + SIDE, SIDE)


def kernel(
    cd_hbm, ab_hbm, amps_ref, ints_ref, out_ref,
    cd_ref, ab_ref, a_mine, a_all, b_mine, b_other, d_all, peaks, peaks_other, rows_up, scales, a_now, partial,
    b_send, b_recv, d_send, d_recv, a_send, a_recv, s_send, s_recv, here_sem,
):
    row, col = lax.axis_index("row"), lax.axis_index("col")
    y, x = row // SIDE, lax.rem(row, SIDE)
    z, core = col // 2, lax.rem(col, 2)
    other = 1 - core
    ids = lambda yy, xx, zz, cc: (yy * SIDE + xx, zz * 2 + cc)
    across = ids(ring(y, 2), x, z, core)
    up_y, down_y = ids(ring(y, 1), x, z, core), ids(ring(y, -1), x, z, core)
    up_x, down_x = ids(y, ring(x, 1), z, core), ids(y, ring(x, -1), z, core)
    up_z, down_z = ids(y, x, ring(z, 1), core), ids(y, x, ring(z, -1), core)
    sibling = ids(y, x, z, other)
    everyone_z = [ids(y, x, ring(z, s), core) for s in (1, 2, 3)]
    everyone_z += [ids(y, x, ring(z, s), other) for s in (0, 1, 2, 3)]
    near = [across, up_y, down_y, up_x, down_x, *everyone_z]

    barrier = pltpu.get_barrier_semaphore()
    for device in near:
        pl.semaphore_signal(barrier, inc=1, device_id=device, device_id_type=MESH)
    loads = [
        pltpu.make_async_copy(source, target, here_sem.at[n])
        for n, (source, target) in enumerate(
            ((amps_ref, a_mine), (ab_hbm, ab_ref), (cd_hbm, cd_ref), (ints_ref, b_mine))
        )
    ]
    for load in loads:
        load.start()

    def remote(source, target, send, recv, device):
        return pltpu.make_async_remote_copy(
            src_ref=source, dst_ref=target, send_sem=send, recv_sem=recv, device_id=device, device_id_type=MESH
        )

    low, high, whole = pl.ds(0, DEPTH // 2), pl.ds(DEPTH // 2, DEPTH // 2), pl.ds(0, DEPTH)
    halves = (low, high)

    def b_copy(g, h):
        return remote(
            ints_ref.at[g, halves[h]], b_other.at[g, halves[h]], b_send.at[g, h], b_recv.at[g, h], across
        )

    slot = lambda s, c: ring(z, s) * 2 + c
    d_kinds = [
        (slot(0, core), low, up_z, slot(-1, core)),
        (slot(0, core), high, up_z, slot(-1, core)),
        (slot(0, core), low, down_z, slot(1, core)),
        (slot(0, core), high, down_z, slot(1, core)),
        (slot(-1, core), low, up_z, slot(2, core)),
        (slot(1, core), high, down_z, slot(2, core)),
        (slot(0, core), whole, sibling, slot(0, other)),
        (slot(-1, core), whole, sibling, slot(-1, other)),
        (slot(1, core), whole, sibling, slot(1, other)),
        (slot(2, core), whole, sibling, slot(2, other)),
    ]

    def d_copy(g, kind, arriving=False):
        leaves, rows, device, fills = d_kinds[kind]
        place = d_all.at[g, fills if arriving else leaves, rows]
        return remote(place, place, d_send.at[g, kind], d_recv.at[g, kind], device)

    first, second, every = pl.ds(0, OCC // 2), pl.ds(OCC // 2, OCC // 2), pl.ds(0, OCC)
    block = lambda sy, sx: ring(y, sy) * SIDE + ring(x, sx)
    a_kinds = [
        (block(0, 0), every, up_y, block(-1, 0)),
        (block(0, 0), every, down_y, block(1, 0)),
        (block(-1, 0), first, up_y, block(2, 0)),
        (block(1, 0), second, down_y, block(2, 0)),
    ]
    for sy in (0, -1, 1, 2):
        a_kinds += [
            (block(sy, 0), every, up_x, block(sy, -1)),
            (block(sy, 0), every, down_x, block(sy, 1)),
            (block(sy, -1), first, up_x, block(sy, 2)),
            (block(sy, 1), second, down_x, block(sy, 2)),
        ]

    def a_copy(p, kind, arriving=False):
        leaves, rows, device, fills = a_kinds[kind]
        place = a_all.at[p, fills if arriving else leaves, rows]
        return remote(place, place, a_send.at[p, kind], a_recv.at[p, kind], device)

    def s_copy(n, mine):
        return remote(scales.at[mine], scales.at[mine], s_send.at[n], s_recv.at[n], everyone_z[n])

    def send_b(g):
        b_copy(g, 0).start()
        b_copy(g, 1).start()

    def moves(p, waits, starts):
        for kind in waits:
            a_copy(p, kind, True).wait_recv()
        for kind in starts:
            a_copy(p, kind).start()

    def passes(g, waits, kind):
        for arrived in waits:
            d_copy(g, arrived, True).wait_recv()
        d_copy(g, kind).start()

    lane = lax.broadcasted_iota(jnp.int32, (DEPTH // 2, DEPTH), 1)
    depth_at = col * DEPTH + lax.broadcasted_iota(jnp.int32, (DEPTH // 2, WIDTH), 0)
    place_at = lax.rem(row, SIDE * SIDE // 2) * WIDTH + lax.broadcasted_iota(jnp.int32, (DEPTH // 2, WIDTH), 1)

    def form(g, h):
        ups = jnp.sum(jnp.where(lane == g, rows_up[halves[h], :], 0.0), axis=1, keepdims=True) * 32768.0
        b_copy(g, h).wait_recv()
        mine, theirs = b_mine[g, halves[h], :], b_other[g, halves[h], :]
        difference = mine.astype(jnp.float32) - theirs.astype(jnp.float32)
        keep = (depth_at < cd_ref[g] - h * (DEPTH // 2)) & (place_at < ab_ref[g])
        scaled = jnp.where(keep, difference * ups, 0.0)
        whole_number = jnp.round(jnp.minimum(scaled, 32767.0)).astype(jnp.int32)
        d_all[g, col, halves[h], :] = whole_number.astype(jnp.int16)
        d_copy(g, h).start()
        d_copy(g, 2 + h).start()
        if h == 1:
            d_copy(g, 6).start()

    does = {
        "form": form,
        "send_b": send_b,
        "own_x": lambda p: moves(p, (), (4, 5)),
        "own_y": lambda p: moves(p, (), (0, 1)),
        "up_y": lambda p: moves(p, (0,), (2, 8, 9)),
        "down_y": lambda p: moves(p, (1,), (3, 12, 13)),
        "far_y": lambda p: moves(p, (2, 3), (16, 17)),
        "on_x": lambda p, kind: moves(p, (kind,), (kind + 2,)),
        "up_z": lambda g: passes(g, (0,), 4),
        "down_z": lambda g: passes(g, (3,), 5),
        "share_up": lambda g: passes(g, (1,), 7),
        "share_down": lambda g: passes(g, (2,), 8),
        "share_far": lambda g: passes(g, (4, 5), 9),
    }

    half = lax.broadcasted_iota(jnp.int32, (OCC, DEPTH), 1) < DEPTH // 2
    chips = (0, -1, 1, 2)

    def product(g, groups, at):
        d = jnp.concatenate(
            [d_all[g, pl.ds(2 * ring(z, chips[i]), 2), :, at].reshape(GROUP, TILE) for i in groups], axis=0
        ).astype(jnp.float32)
        top = d.astype(jnp.bfloat16)
        rest = (d - top.astype(jnp.float32)).astype(jnp.bfloat16)
        a = a_now[:, groups[0] * GROUP : (groups[-1] + 1) * GROUP]
        summed = jnp.dot(a, top, preferred_element_type=jnp.float32)
        summed += jnp.dot(a, rest, preferred_element_type=jnp.float32)
        return summed * (1.0 / 32768.0)

    def gather(g):
        p, parity = g // 2, lax.rem(g, 2)

        @pl.when(parity == 0)
        def _():
            for kind in (6, 7, 10, 11, 14, 15, 18, 19):
                a_copy(p, kind, True).wait_recv()

        for kind in (6, 7, 8):
            d_copy(g, kind, True).wait_recv()
        for i in range(SIDE):
            for c in (0, 1):
                m = 2 * ring(z, chips[i]) + c
                left = pltpu.roll(a_all[p, 2 * m].astype(jnp.float32), 64 * parity, 1)
                right = pltpu.roll(a_all[p, 2 * m + 1].astype(jnp.float32), 64 - 64 * parity, 1)
                joined = jnp.where(half, left, right) * scales[m, pl.ds(g, 1), :]
                k = (2 * i + c) * DEPTH
                a_now[:, k : k + DEPTH] = joined.astype(jnp.bfloat16)

    def strip(n):
        return pl.ds(pl.multiple_of(n * TILE, TILE), TILE)

    def multiply_most(g, n):
        partial[n] = product(g, (0, 1, 2), strip(n))

    def multiply_rest(g, n):
        out_ref[g, :, strip(n)] = (partial[n] + product(g, (3,), strip(n))).astype(jnp.bfloat16)

    for load in loads[1:]:
        load.wait()

    def peak(g, _):
        most = []
        for h in (0, 1):
            size = jnp.abs(b_mine[g, halves[h], :].astype(jnp.float32))
            size = jnp.where(place_at < ab_ref[g], size, 0.0)
            most.append(jnp.max(size, axis=1, keepdims=True))
        spread = jnp.broadcast_to(jnp.concatenate(most, axis=0), (DEPTH, DEPTH))
        peaks[pl.ds(g, 1), :] = jnp.transpose(spread)[0:1, :]
        return 0

    lax.fori_loop(0, IRREPS, peak, 0)
    pl.semaphore_wait(barrier, len(near))
    peak_copy = remote(peaks, peaks_other, s_send.at[7], s_recv.at[7], across)
    peak_copy.start()
    send_b(0)
    loads[0].wait()
    for p in range(PAIRS):
        a_all[p, row] = jnp.transpose(a_mine[p].astype(jnp.float32)).astype(jnp.bfloat16)
        if p == 0:
            moves(0, (), (4, 5, 0, 1))
    peak_copy.wait_recv()
    left = peaks[...] + peaks_other[...]
    up, down = jnp.ones_like(left), jnp.ones_like(left)
    for power in (32, 16, 8, 4, 2, 1):
        small = left < 2.0**-power
        left = jnp.where(small, left * 2.0**power, left)
        up = jnp.where(small, up * 2.0**power, up)
        down = jnp.where(small, down * 2.0**-power, down)
    rows_up[...] = jnp.transpose(jnp.concatenate([up] * 16, axis=0))
    scales[col] = down
    for n in range(7):
        s_copy(n, col).start()

    def unit(i, _):
        for at, calls in PLAN.items():
            @pl.when(i == at)
            def _(calls=calls):
                for name, *where in calls:
                    does[name](*where)

        @pl.when(i == 0)
        def _():
            sender = [slot(-1, core), slot(-2, core), slot(-3, core)] + [slot(-n, other) for n in (0, 1, 2, 3)]
            for n in range(7):
                s_copy(n, sender[n]).wait_recv()

        g, n = i // STRIPS, lax.rem(i, STRIPS)
        last = IRREPS * STRIPS

        @pl.when(i < last)
        def _():
            pl.when(n == 0)(lambda: gather(g))
            multiply_most(g, n)

        @pl.when((i < last - STRIPS) | (i >= last))
        def _():
            block = g - i // last
            pl.when(n == 0)(lambda: d_copy(block, 9, True).wait_recv())
            multiply_rest(block, n)

        return 0

    lax.fori_loop(0, UNITS, unit, 0)

    for n in range(7):
        s_copy(n, col).wait_send()
    peak_copy.wait_send()

    def drain_b(g, _):
        b_copy(g, 0).wait_send()
        b_copy(g, 1).wait_send()
        for kind in range(D_KINDS):
            d_copy(g, kind).wait_send()
        return 0

    def drain_a(p, _):
        for kind in range(A_KINDS):
            a_copy(p, kind).wait_send()
        return 0

    lax.fori_loop(0, IRREPS, drain_b, 0)
    lax.fori_loop(0, PAIRS, drain_a, 0)


def interleave(in_ref, out_ref, given, out_sem):
    def give(n):
        rows = pl.ds(pl.multiple_of(n * (SLAB * IRREPS), SLAB * IRREPS), SLAB * IRREPS)
        return pltpu.make_async_copy(given.at[n], out_ref.at[rows], out_sem.at[n])

    def slab(n, _):
        rows = pl.ds(pl.multiple_of(n * SLAB, SLAB), SLAB)
        given[n] = jnp.swapaxes(in_ref[:, rows, :], 0, 1).reshape(SLAB * IRREPS, WIDTH)
        give(n).start()
        return 0

    slabs = OCC // SLAB
    lax.fori_loop(0, slabs, slab, 0)
    for n in range(slabs):
        give(n).wait()


def per_device(amplitudes, integrals, cd_count, ab_count):
    pairs = amplitudes.transpose(1, 2, 0).reshape(PAIRS, DEPTH, OCC)
    by_irrep = pl.pallas_call(
        kernel,
        out_shape=pltpu.VMEM((IRREPS, OCC, WIDTH), jnp.bfloat16),
        in_specs=[pl.BlockSpec(memory_space=pltpu.HBM)] * 4,
        out_specs=pl.BlockSpec(memory_space=pltpu.VMEM),
        scratch_shapes=[
            pltpu.SMEM((IRREPS,), jnp.int32),
            pltpu.SMEM((IRREPS,), jnp.int32),
            pltpu.VMEM((PAIRS, DEPTH, OCC), jnp.bfloat16),
            pltpu.VMEM((PAIRS, 16, OCC, DEPTH), jnp.bfloat16),
            pltpu.VMEM((IRREPS, DEPTH, WIDTH), jnp.bfloat16),
            pltpu.VMEM((IRREPS, DEPTH, WIDTH), jnp.bfloat16),
            pltpu.VMEM((IRREPS, 8, DEPTH, WIDTH), jnp.int16),
            pltpu.VMEM((IRREPS, DEPTH), jnp.float32),
            pltpu.VMEM((IRREPS, DEPTH), jnp.float32),
            pltpu.VMEM((DEPTH, DEPTH), jnp.float32),
            pltpu.VMEM((8, IRREPS, DEPTH), jnp.float32),
            pltpu.VMEM((OCC, 8 * DEPTH), jnp.bfloat16),
            pltpu.VMEM((STRIPS, OCC, TILE), jnp.float32),
            pltpu.SemaphoreType.DMA((IRREPS, 2)),
            pltpu.SemaphoreType.DMA((IRREPS, 2)),
            pltpu.SemaphoreType.DMA((IRREPS, D_KINDS)),
            pltpu.SemaphoreType.DMA((IRREPS, D_KINDS)),
            pltpu.SemaphoreType.DMA((PAIRS, A_KINDS)),
            pltpu.SemaphoreType.DMA((PAIRS, A_KINDS)),
            pltpu.SemaphoreType.DMA((8,)),
            pltpu.SemaphoreType.DMA((8,)),
            pltpu.SemaphoreType.DMA((4,)),
        ],
        compiler_params=pltpu.CompilerParams(
            collective_id=0, has_side_effects=True, vmem_limit_bytes=48 << 20
        ),
        cost_estimate=pl.CostEstimate(flops=17 << 30, bytes_accessed=12 << 20, transcendentals=0),
    )(*(pltpu.with_memory_space_constraint(v, pltpu.HBM) for v in (cd_count, ab_count, pairs, integrals)))
    slabs = OCC // SLAB
    ladder = pl.pallas_call(
        interleave,
        out_shape=jax.ShapeDtypeStruct((OCC * IRREPS, WIDTH), jnp.bfloat16),
        in_specs=[pl.BlockSpec(memory_space=pltpu.VMEM)],
        out_specs=pl.BlockSpec(memory_space=pl.ANY),
        scratch_shapes=[
            pltpu.VMEM((slabs, SLAB * IRREPS, WIDTH), jnp.bfloat16),
            pltpu.SemaphoreType.DMA((slabs,)),
        ],
        compiler_params=pltpu.CompilerParams(vmem_limit_bytes=16 << 20),
    )(pltpu.with_memory_space_constraint(by_irrep, pltpu.VMEM))
    return ladder.reshape(OCC, IRREPS, WIDTH)


def solution(mesh):
    in_specs = (P("col", None, "row"), P(None, "col", "row"), P(), P())
    out_specs = P("col", None, "row")
    return jax.shard_map(
        per_device, mesh=mesh, in_specs=in_specs, out_specs=out_specs, check_vma=False
    )
```

```python
import functools

import jax
import jax.numpy as jnp
from jax import lax
from jax.experimental import pallas as pl
from jax.experimental.pallas import tpu as pltpu
from jax.sharding import PartitionSpec as P

MESH = pl.DeviceIdType.MESH
IRREPS = 8
PAIRS = 4
SIDE = 4
OCC = 512
DEPTH = 128
WIDTH = 1024
NABG = 8192
TILE = 1024
D_KINDS = 10
A_KINDS = 20
UNITS = 9
STRIPS = 1
SLAB = 32
GROUP = 2 * DEPTH

PLAN = {
    0: [
        ("own_x", 1), ("send_b", 1), ("own_x", 2), ("on_x", 0, 4), ("on_x", 0, 5),
        ("form", 0, 0), ("on_x", 1, 4), ("on_x", 1, 5), ("send_b", 2), ("form", 0, 1),
        ("own_x", 3), ("up_y", 0), ("down_y", 0), ("on_x", 2, 4), ("on_x", 2, 5),
        ("up_z", 0), ("form", 1, 0), ("share_up", 0), ("down_z", 0), ("share_down", 0),
        ("own_y", 1), ("on_x", 3, 4), ("on_x", 3, 5), ("form", 1, 1), ("send_b", 3),
        ("on_x", 0, 8), ("on_x", 0, 9), ("form", 2, 0), ("up_z", 1), ("on_x", 0, 12),
        ("on_x", 0, 13), ("form", 2, 1), ("share_far", 0), ("share_up", 1), ("far_y", 0),
        ("send_b", 4), ("down_z", 1), ("share_down", 1), ("up_z", 2), ("up_y", 1),
        ("down_y", 1), ("form", 3, 0), ("on_x", 0, 16), ("on_x", 0, 17), ("own_y", 2),
        ("down_z", 2), ("share_down", 2), ("share_up", 2), ("form", 3, 1), ("on_x", 1, 8),
        ("on_x", 1, 9), ("send_b", 5), ("share_far", 1), ("form", 4, 0), ("on_x", 1, 12),
        ("on_x", 1, 13), ("up_z", 3),
    ],
    1: [
        ("form", 4, 1), ("far_y", 1), ("share_far", 2), ("share_up", 3), ("up_y", 2),
        ("down_y", 2), ("down_z", 3), ("share_down", 3), ("up_z", 4), ("send_b", 6),
    ],
    2: [
        ("form", 5, 0), ("own_y", 3), ("on_x", 1, 16), ("on_x", 1, 17), ("form", 5, 1),
        ("down_z", 4), ("share_down", 4), ("share_up", 4), ("far_y", 2), ("send_b", 7),
        ("on_x", 2, 8), ("on_x", 2, 9), ("share_far", 3), ("form", 6, 0), ("on_x", 2, 12),
        ("on_x", 2, 13), ("up_z", 5),
    ],
    3: [
        ("form", 6, 1), ("down_z", 5), ("share_down", 5), ("share_up", 5), ("on_x", 2, 16),
        ("on_x", 2, 17), ("up_y", 3), ("down_y", 3),
    ],
    4: [
        ("share_far", 4), ("up_z", 6), ("form", 7, 0), ("form", 7, 1), ("far_y", 3),
        ("down_z", 6), ("share_down", 6), ("share_up", 6), ("on_x", 3, 8), ("on_x", 3, 9),
    ],
    5: [
        ("share_far", 5), ("on_x", 3, 12), ("on_x", 3, 13), ("up_z", 7), ("on_x", 3, 16),
        ("on_x", 3, 17),
    ],
    6: [
        ("down_z", 7), ("share_down", 7), ("share_up", 7), ("share_far", 6),
    ],
    7: [
        ("share_far", 7),
    ],
}


def ring(value, step):
    return lax.rem(value + step + SIDE, SIDE)


def kernel(
    cd_hbm, ab_hbm, amps_ref, ints_ref, out_ref,
    cd_ref, ab_ref, a_mine, a_all, b_mine, b_other, d_all, peaks, peaks_other, rows_up, scales, a_now, partial,
    b_send, b_recv, d_send, d_recv, a_send, a_recv, s_send, s_recv, here_sem,
):
    row, col = lax.axis_index("row"), lax.axis_index("col")
    y, x = row // SIDE, lax.rem(row, SIDE)
    z, core = col // 2, lax.rem(col, 2)
    other = 1 - core
    ids = lambda yy, xx, zz, cc: (yy * SIDE + xx, zz * 2 + cc)
    across = ids(ring(y, 2), x, z, core)
    up_y, down_y = ids(ring(y, 1), x, z, core), ids(ring(y, -1), x, z, core)
    up_x, down_x = ids(y, ring(x, 1), z, core), ids(y, ring(x, -1), z, core)
    up_z, down_z = ids(y, x, ring(z, 1), core), ids(y, x, ring(z, -1), core)
    sibling = ids(y, x, z, other)
    everyone_z = [ids(y, x, ring(z, s), core) for s in (1, 2, 3)]
    everyone_z += [ids(y, x, ring(z, s), other) for s in (0, 1, 2, 3)]
    near = [across, up_y, down_y, up_x, down_x, *everyone_z]

    barrier = pltpu.get_barrier_semaphore()
    for device in near:
        pl.semaphore_signal(barrier, inc=1, device_id=device, device_id_type=MESH)
    loads = [
        pltpu.make_async_copy(source, target, here_sem.at[n])
        for n, (source, target) in enumerate(
            ((amps_ref, a_mine), (ab_hbm, ab_ref), (cd_hbm, cd_ref), (ints_ref, b_mine))
        )
    ]
    for load in loads:
        load.start()

    def remote(source, target, send, recv, device):
        return pltpu.make_async_remote_copy(
            src_ref=source, dst_ref=target, send_sem=send, recv_sem=recv, device_id=device, device_id_type=MESH
        )

    low, high, whole = pl.ds(0, DEPTH // 2), pl.ds(DEPTH // 2, DEPTH // 2), pl.ds(0, DEPTH)
    halves = (low, high)

    def b_copy(g, h):
        return remote(
            ints_ref.at[g, halves[h]], b_other.at[g, halves[h]], b_send.at[g, h], b_recv.at[g, h], across
        )

    slot = lambda s, c: ring(z, s) * 2 + c
    d_kinds = [
        (slot(0, core), low, up_z, slot(-1, core)),
        (slot(0, core), high, up_z, slot(-1, core)),
        (slot(0, core), low, down_z, slot(1, core)),
        (slot(0, core), high, down_z, slot(1, core)),
        (slot(-1, core), low, up_z, slot(2, core)),
        (slot(1, core), high, down_z, slot(2, core)),
        (slot(0, core), whole, sibling, slot(0, other)),
        (slot(-1, core), whole, sibling, slot(-1, other)),
        (slot(1, core), whole, sibling, slot(1, other)),
        (slot(2, core), whole, sibling, slot(2, other)),
    ]

    def d_copy(g, kind, arriving=False):
        leaves, rows, device, fills = d_kinds[kind]
        place = d_all.at[g, fills if arriving else leaves, rows]
        return remote(place, place, d_send.at[g, kind], d_recv.at[g, kind], device)

    first, second, every = pl.ds(0, OCC // 2), pl.ds(OCC // 2, OCC // 2), pl.ds(0, OCC)
    block = lambda sy, sx: ring(y, sy) * SIDE + ring(x, sx)
    a_kinds = [
        (block(0, 0), every, up_y, block(-1, 0)),
        (block(0, 0), every, down_y, block(1, 0)),
        (block(-1, 0), first, up_y, block(2, 0)),
        (block(1, 0), second, down_y, block(2, 0)),
    ]
    for sy in (0, -1, 1, 2):
        a_kinds += [
            (block(sy, 0), every, up_x, block(sy, -1)),
            (block(sy, 0), every, down_x, block(sy, 1)),
            (block(sy, -1), first, up_x, block(sy, 2)),
            (block(sy, 1), second, down_x, block(sy, 2)),
        ]

    def a_copy(p, kind, arriving=False):
        leaves, rows, device, fills = a_kinds[kind]
        place = a_all.at[p, fills if arriving else leaves, rows]
        return remote(place, place, a_send.at[p, kind], a_recv.at[p, kind], device)

    def s_copy(n, mine):
        return remote(scales.at[mine], scales.at[mine], s_send.at[n], s_recv.at[n], everyone_z[n])

    def send_b(g):
        b_copy(g, 0).start()
        b_copy(g, 1).start()

    def moves(p, waits, starts):
        for kind in waits:
            a_copy(p, kind, True).wait_recv()
        for kind in starts:
            a_copy(p, kind).start()

    def passes(g, waits, kind):
        for arrived in waits:
            d_copy(g, arrived, True).wait_recv()
        d_copy(g, kind).start()

    lane = lax.broadcasted_iota(jnp.int32, (DEPTH // 2, DEPTH), 1)
    depth_at = col * DEPTH + lax.broadcasted_iota(jnp.int32, (DEPTH // 2, WIDTH), 0)
    place_at = lax.rem(row, SIDE * SIDE // 2) * WIDTH + lax.broadcasted_iota(jnp.int32, (DEPTH // 2, WIDTH), 1)

    def form(g, h):
        ups = jnp.sum(jnp.where(lane == g, rows_up[halves[h], :], 0.0), axis=1, keepdims=True) * 32768.0
        b_copy(g, h).wait_recv()
        mine, theirs = b_mine[g, halves[h], :], b_other[g, halves[h], :]
        difference = mine.astype(jnp.float32) - theirs.astype(jnp.float32)
        keep = (depth_at < cd_ref[g] - h * (DEPTH // 2)) & (place_at < ab_ref[g])
        scaled = jnp.where(keep, difference * ups, 0.0)
        whole_number = jnp.round(jnp.minimum(scaled, 32767.0)).astype(jnp.int32)
        d_all[g, col, halves[h], :] = whole_number.astype(jnp.int16)
        d_copy(g, h).start()
        if g == 0:
            d_copy(g, 2 + h).start()
        elif h == 1:
            d_copy(g, 3).start()
            d_copy(g, 2).start()
        if h == 1:
            d_copy(g, 6).start()

    does = {
        "form": form,
        "send_b": send_b,
        "own_x": lambda p: moves(p, (), (4, 5)),
        "own_y": lambda p: moves(p, (), (0, 1)),
        "up_y": lambda p: moves(p, (0,), (2, 8, 9)),
        "down_y": lambda p: moves(p, (1,), (3, 12, 13)),
        "far_y": lambda p: moves(p, (2, 3), (16, 17)),
        "on_x": lambda p, kind: moves(p, (kind,), (kind + 2,)),
        "up_z": lambda g: passes(g, (0,), 4),
        "down_z": lambda g: passes(g, (3,), 5),
        "share_up": lambda g: passes(g, (1,), 7),
        "share_down": lambda g: passes(g, (2,), 8),
        "share_far": lambda g: passes(g, (4, 5), 9),
    }

    half = lax.broadcasted_iota(jnp.int32, (OCC, DEPTH), 1) < DEPTH // 2
    chips = (0, -1, 1, 2)

    def product(g, groups, at):
        d = jnp.concatenate(
            [d_all[g, pl.ds(2 * ring(z, chips[i]), 2), :, at].reshape(GROUP, TILE) for i in groups], axis=0
        ).astype(jnp.float32)
        top = d.astype(jnp.bfloat16)
        rest = (d - top.astype(jnp.float32)).astype(jnp.bfloat16)
        a = a_now[:, groups[0] * GROUP : (groups[-1] + 1) * GROUP]
        summed = jnp.dot(a, top, preferred_element_type=jnp.float32)
        summed += jnp.dot(a, rest, preferred_element_type=jnp.float32)
        return summed * (1.0 / 32768.0)

    def gather(g):
        p, parity = g // 2, lax.rem(g, 2)

        @pl.when(parity == 0)
        def _():
            for kind in (6, 7, 10, 11, 14, 15, 18, 19):
                a_copy(p, kind, True).wait_recv()

        for kind in (6, 7, 8):
            d_copy(g, kind, True).wait_recv()
        for i in range(SIDE):
            for c in (0, 1):
                m = 2 * ring(z, chips[i]) + c
                left = pltpu.roll(a_all[p, 2 * m].astype(jnp.float32), 64 * parity, 1)
                right = pltpu.roll(a_all[p, 2 * m + 1].astype(jnp.float32), 64 - 64 * parity, 1)
                joined = jnp.where(half, left, right) * scales[m, pl.ds(g, 1), :]
                k = (2 * i + c) * DEPTH
                a_now[:, k : k + DEPTH] = joined.astype(jnp.bfloat16)

    def strip(n):
        return pl.ds(pl.multiple_of(n * TILE, TILE), TILE)

    def multiply_most(g, n):
        partial[n] = product(g, (0, 1, 2), strip(n))

    def multiply_rest(g, n):
        out_ref[g, :, strip(n)] = (partial[n] + product(g, (3,), strip(n))).astype(jnp.bfloat16)

    for load in loads[1:]:
        load.wait()

    def peak(g, _):
        most = []
        for h in (0, 1):
            size = jnp.abs(b_mine[g, halves[h], :].astype(jnp.float32))
            size = jnp.where(place_at < ab_ref[g], size, 0.0)
            most.append(jnp.max(size, axis=1, keepdims=True))
        spread = jnp.broadcast_to(jnp.concatenate(most, axis=0), (DEPTH, DEPTH))
        peaks[pl.ds(g, 1), :] = jnp.transpose(spread)[0:1, :]
        return 0

    lax.fori_loop(0, IRREPS, peak, 0)
    pl.semaphore_wait(barrier, len(near))
    peak_copy = remote(peaks, peaks_other, s_send.at[7], s_recv.at[7], across)
    peak_copy.start()
    send_b(0)
    loads[0].wait()
    for p in range(PAIRS):
        a_all[p, row] = jnp.transpose(a_mine[p].astype(jnp.float32)).astype(jnp.bfloat16)
        if p == 0:
            moves(0, (), (4, 5, 0, 1))
    peak_copy.wait_recv()
    left = peaks[...] + peaks_other[...]
    up, down = jnp.ones_like(left), jnp.ones_like(left)
    for power in (32, 16, 8, 4, 2, 1):
        small = left < 2.0**-power
        left = jnp.where(small, left * 2.0**power, left)
        up = jnp.where(small, up * 2.0**power, up)
        down = jnp.where(small, down * 2.0**-power, down)
    rows_up[...] = jnp.transpose(jnp.concatenate([up] * 16, axis=0))
    scales[col] = down
    for n in range(7):
        s_copy(n, col).start()

    def sent_blocks(g, kinds=D_KINDS):
        b_copy(g, 0).wait_send()
        b_copy(g, 1).wait_send()
        for kind in range(kinds):
            d_copy(g, kind).wait_send()

    def sent_pair(p):
        for kind in range(A_KINDS):
            a_copy(p, kind).wait_send()

    def unit(i, _):
        for at, calls in PLAN.items():
            @pl.when(i == at)
            def _(calls=calls):
                for name, *where in calls:
                    does[name](*where)

        @pl.when(i == 0)
        def _():
            sender = [slot(-1, core), slot(-2, core), slot(-3, core)] + [slot(-n, other) for n in (0, 1, 2, 3)]
            for n in range(7):
                s_copy(n, sender[n]).wait_recv()
                s_copy(n, col).wait_send()
            peak_copy.wait_send()

        pl.when((i >= 2) & (i < IRREPS))(lambda: sent_blocks(i - 2))
        pl.when((i >= 3) & (i < IRREPS) & (lax.rem(i, 2) == 1))(lambda: sent_pair((i - 3) // 2))

        @pl.when(i == IRREPS)
        def _():
            sent_blocks(IRREPS - 2)
            sent_pair(PAIRS - 1)
            sent_blocks(IRREPS - 1, D_KINDS - 1)

        g, n = i // STRIPS, lax.rem(i, STRIPS)
        last = IRREPS * STRIPS

        @pl.when(i < last)
        def _():
            pl.when(n == 0)(lambda: gather(g))
            multiply_most(g, n)

        @pl.when((i < last - STRIPS) | (i >= last))
        def _():
            block = g - i // last
            pl.when(n == 0)(lambda: d_copy(block, 9, True).wait_recv())
            multiply_rest(block, n)

        return 0

    lax.fori_loop(0, UNITS, unit, 0)

    d_copy(IRREPS - 1, D_KINDS - 1).wait_send()


def interleave(in_ref, out_ref, given, out_sem):
    def give(n):
        rows = pl.ds(pl.multiple_of(n * (SLAB * IRREPS), SLAB * IRREPS), SLAB * IRREPS)
        return pltpu.make_async_copy(given.at[n], out_ref.at[rows], out_sem.at[n])

    def slab(n, _):
        rows = pl.ds(pl.multiple_of(n * SLAB, SLAB), SLAB)
        given[n] = jnp.swapaxes(in_ref[:, rows, :], 0, 1).reshape(SLAB * IRREPS, WIDTH)
        give(n).start()
        return 0

    slabs = OCC // SLAB
    lax.fori_loop(0, slabs, slab, 0)
    for n in range(slabs):
        give(n).wait()


def per_device(amplitudes, integrals, cd_count, ab_count):
    pairs = amplitudes.transpose(1, 2, 0).reshape(PAIRS, DEPTH, OCC)
    by_irrep = pl.pallas_call(
        kernel,
        out_shape=pltpu.VMEM((IRREPS, OCC, WIDTH), jnp.bfloat16),
        in_specs=[pl.BlockSpec(memory_space=pltpu.HBM)] * 4,
        out_specs=pl.BlockSpec(memory_space=pltpu.VMEM),
        scratch_shapes=[
            pltpu.SMEM((IRREPS,), jnp.int32),
            pltpu.SMEM((IRREPS,), jnp.int32),
            pltpu.VMEM((PAIRS, DEPTH, OCC), jnp.bfloat16),
            pltpu.VMEM((PAIRS, 16, OCC, DEPTH), jnp.bfloat16),
            pltpu.VMEM((IRREPS, DEPTH, WIDTH), jnp.bfloat16),
            pltpu.VMEM((IRREPS, DEPTH, WIDTH), jnp.bfloat16),
            pltpu.VMEM((IRREPS, 8, DEPTH, WIDTH), jnp.int16),
            pltpu.VMEM((IRREPS, DEPTH), jnp.float32),
            pltpu.VMEM((IRREPS, DEPTH), jnp.float32),
            pltpu.VMEM((DEPTH, DEPTH), jnp.float32),
            pltpu.VMEM((8, IRREPS, DEPTH), jnp.float32),
            pltpu.VMEM((OCC, 8 * DEPTH), jnp.bfloat16),
            pltpu.VMEM((STRIPS, OCC, TILE), jnp.float32),
            pltpu.SemaphoreType.DMA((IRREPS, 2)),
            pltpu.SemaphoreType.DMA((IRREPS, 2)),
            pltpu.SemaphoreType.DMA((IRREPS, D_KINDS)),
            pltpu.SemaphoreType.DMA((IRREPS, D_KINDS)),
            pltpu.SemaphoreType.DMA((PAIRS, A_KINDS)),
            pltpu.SemaphoreType.DMA((PAIRS, A_KINDS)),
            pltpu.SemaphoreType.DMA((8,)),
            pltpu.SemaphoreType.DMA((8,)),
            pltpu.SemaphoreType.DMA((4,)),
        ],
        compiler_params=pltpu.CompilerParams(
            collective_id=0, has_side_effects=True, vmem_limit_bytes=48 << 20
        ),
        cost_estimate=pl.CostEstimate(flops=17 << 30, bytes_accessed=12 << 20, transcendentals=0),
    )(*(pltpu.with_memory_space_constraint(v, pltpu.HBM) for v in (cd_count, ab_count, pairs, integrals)))
    slabs = OCC // SLAB
    ladder = pl.pallas_call(
        interleave,
        out_shape=jax.ShapeDtypeStruct((OCC * IRREPS, WIDTH), jnp.bfloat16),
        in_specs=[pl.BlockSpec(memory_space=pltpu.VMEM)],
        out_specs=pl.BlockSpec(memory_space=pl.ANY),
        scratch_shapes=[
            pltpu.VMEM((slabs, SLAB * IRREPS, WIDTH), jnp.bfloat16),
            pltpu.SemaphoreType.DMA((slabs,)),
        ],
        compiler_params=pltpu.CompilerParams(vmem_limit_bytes=16 << 20),
    )(pltpu.with_memory_space_constraint(by_irrep, pltpu.VMEM))
    return ladder.reshape(OCC, IRREPS, WIDTH)


def solution(mesh):
    in_specs = (P("col", None, "row"), P(None, "col", "row"), P(), P())
    out_specs = P("col", None, "row")
    return jax.shard_map(
        per_device, mesh=mesh, in_specs=in_specs, out_specs=out_specs, check_vma=False
    )
```
